32 devices in a mesh: groups: 2 (over x), expert: 16 (over z, y, core).
Axes of the slice: x: 2, y: 2, z: 4, core: 2. Of those that a mesh axis runs over, the one named last changes fastest.
Arguments:
- frames: bfloat16 [32, 384, 1024], P(('groups', 'expert')), parts along dimension 0, may hold values from -6 to 6
- frame_counts: int32 [32], P(('groups', 'expert')), parts along dimension 0, may hold values from 1 to 384, 4608 in all
- expert_ids: int32 [32, 384, 1], P(('groups', 'expert')), parts along dimension 0, may hold values from 0 to 7
- conv_kernel: float32 [31, 1024], replicated, may hold values from -1 to 1
- router: bfloat16 [1024, 8], replicated, may hold values from -0.1875 to 0.1875
- w_in: bfloat16 [1024, 32768], P(None, 'expert'), may hold values from -0.1875 to 0.1875
- w_out: bfloat16 [32768, 1024], P('expert'), may hold values from -0.09375 to 0.09375
- final_gain: float32 [1024], replicated, may hold values from 0.1 to 1.9
Outputs:
- block_out: bfloat16 [32, 384, 1024], P(('groups', 'expert')), parts along dimension 0
The draws below stay inside these ranges and needn't reach their ends.
There are 2 independent parts, one for each index of `groups`. The reference program is written for one: setup_inputs(seed, part) draws one part's arguments, and reference() takes and returns one part's arrays. A program takes and returns all parts, laid end to end along the dimension named above; an argument that names none is the same for every part. Nothing has to cross between parts.
Inputs may be any that keep to these rules, and one draw needn't show every extreme that they name: `frame_counts`: some utterance of every part uses all 384 frames.
All inputs are finite; a program needn't handle non-finite values. No bound on the sum of `frame_counts` on one device may be relied on, other than what follows from the above.
Results may differ from the reference program's by a relative error of at most 0.0047.
Values may be sent and summed in bfloat16 or wider, within the bound.
No kernel may reach another device: no remote copies, remote signals or barrier semaphores. Data moves between devices by JAX's collectives and lax.ppermute only.
A program may use at most 64 MiB of HBM per device.

```python
import math
import jax
import jax.numpy as jnp
import numpy as np
from jax import lax

D = 1024
FF = 4096
KERNEL = 31
FRAMES = 384
EXPERTS = 8
UTTS = 16
CAP = 60


def levels(stream_key, dims, cuts, smallest, top_value):
    def one(dim, shards_of):
        steps = jax.random.uniform(jax.random.fold_in(jax.random.fold_in(stream_key, 6), dim), (shards_of,), jnp.float32, smallest / len(cuts), top_value / len(cuts))
        return jnp.repeat(jnp.exp(steps), dims[dim] // shards_of).reshape((-1,) + (1,) * (len(dims) - dim - 1))

    level = one(*cuts[0])
    for cut in cuts[1:]:
        level = level * one(*cut)
    return level


def picks_of(key, rows, count, top, lift):
    ranking = jax.random.permutation(jax.random.fold_in(key, 1), count)
    boost = ranking
    for power in range(3):
        boost = boost * boost // count
    boost = boost * lift // count
    tickets = jax.random.randint(jax.random.fold_in(key, 2), (rows, count), 0, 4096) + boost
    sure = jax.random.permutation(jax.random.fold_in(key, 3), rows)[jnp.arange(count) % rows]
    tickets = jnp.where(jnp.arange(rows)[:, None] == sure[None, :], 1 << 14, tickets)
    merit = tickets * count + jnp.arange(count)
    return lax.top_k(merit.astype(jnp.int32), top)[1].astype(jnp.int32)


def length_profile(amount, total, most, skew):
    loads = [(1 << 20) // math.isqrt(standing ** skew) + 1 for standing in range(2, amount + 1)]
    surplus, holding = total - most - (amount - 1), [1] * (amount - 1)
    while surplus > 0:
        movable = [i for i in range(amount - 1) if holding[i] < most]
        whole, left = sum([loads[i] for i in movable]), surplus
        for i in movable:
            addition = min(most - holding[i], max(1, left * loads[i] // whole), surplus)
            holding[i] = holding[i] + addition
            surplus = surplus - addition
    return np.array([most] + holding)


def uneven_parts(own_key, amount, total, most, slope):
    if amount == 2:
        one = jax.random.randint(own_key, (), max(1, total - most), min(most, total - 1) + 1)
        return jnp.stack([one, total - one])
    lengths = jnp.asarray(length_profile(amount, total, most, slope), jnp.int32)
    couples = (amount - 1) // 2
    donor, taker = lengths[1:1 + 2 * couples:2], lengths[2:2 + 2 * couples:2]
    slack = jnp.minimum(donor - 1, most - taker)
    moved = jax.random.randint(jax.random.fold_in(own_key, 1), (couples,), 0, 1 << 20) % (slack + 1)
    lengths = lengths.at[1:1 + 2 * couples:2].set(donor - moved).at[2:2 + 2 * couples:2].set(taker + moved)
    return lengths[jax.random.permutation(jax.random.fold_in(own_key, 2), amount)]


def gaussian(key, dims, deviation, limit, pieces=(), kind=jnp.bfloat16):
    array = deviation * jax.random.normal(key, dims, jnp.float32)
    if pieces:
        array = array * levels(key, dims, pieces, -0.22, 0.18)
    return jnp.clip(array, -limit, limit).astype(kind)


def setup_inputs(seed: int = 0, part: int = 0) -> dict:
    keys = jax.random.split(jax.random.key(seed), 9)
    part_keys = jax.random.split(jax.random.fold_in(keys[8], part), 9)
    frames = gaussian(part_keys[0], (UTTS, FRAMES, D), 1.0, 6.0, ((0, 16),))
    frame_counts = uneven_parts(part_keys[1], UTTS, UTTS * FRAMES * 3 // 4, FRAMES, 0).astype(jnp.int32)
    expert_ids = picks_of(part_keys[2], UTTS * FRAMES, EXPERTS, 1, 1024).reshape((UTTS, FRAMES, 1))
    conv_kernel = gaussian(keys[3], (KERNEL, D), KERNEL ** -0.5, 1.0, (), jnp.float32)
    router = gaussian(keys[4], (D, EXPERTS), D ** -0.5, 0.1875)
    w_in = gaussian(keys[5], (D, EXPERTS * FF), D ** -0.5, 0.1875, ((1, 16),))
    w_out = gaussian(keys[6], (EXPERTS * FF, D), FF ** -0.5, 0.09375, ((0, 16),))
    final_gain = jnp.clip(1.0 + 0.18 * jax.random.normal(keys[7], (D,), jnp.float32), 0.1, 1.9)
    return dict(frames=frames, frame_counts=frame_counts, expert_ids=expert_ids, conv_kernel=conv_kernel, router=router, w_in=w_in, w_out=w_out, final_gain=final_gain)


def layer_norm(values):
    mean = lax.optimization_barrier(jnp.mean(values, axis=-1, keepdims=True))
    centred = values - mean
    variance = lax.optimization_barrier(jnp.mean(centred * centred, axis=-1, keepdims=True))
    return centred * lax.rsqrt(variance + 1e-05)

def reference(frames, frame_counts, expert_ids, conv_kernel, router, w_in, w_out, final_gain):
    positions = jnp.arange(FRAMES, dtype=jnp.int32)
    valid = positions[None, :] < frame_counts[:, None]
    inputs = frames.astype(jnp.float32)
    normed = layer_norm(inputs) * valid[..., None].astype(jnp.float32)
    reach = KERNEL // 2
    padded = jnp.pad(normed, ((0, 0), (reach, reach), (0, 0)))
    conv = jnp.zeros_like(normed)
    for step in range(KERNEL):
        conv = conv + conv_kernel[step][None, None, :] * padded[:, step:step + FRAMES, :]
    stream = (inputs + jax.nn.silu(conv)).astype(jnp.bfloat16)
    expert_in = layer_norm(stream.astype(jnp.float32)).astype(jnp.bfloat16)
    logits = jnp.einsum('utd,de->ute', expert_in.astype(jnp.float32), router.astype(jnp.float32))
    chosen_ids = expert_ids[..., 0]
    onehot = ((chosen_ids[..., None] == jnp.arange(EXPERTS, dtype=jnp.int32)) & valid[..., None]).astype(jnp.int32)
    before = jnp.cumsum(onehot, axis=1) - onehot
    rank = lax.optimization_barrier(jnp.sum(before * onehot, axis=-1))
    gate = jax.nn.sigmoid(lax.optimization_barrier(jnp.sum(logits * onehot.astype(jnp.float32), axis=-1)))
    sent = valid & (rank < CAP)
    slot = jnp.minimum(rank, CAP - 1)
    utter = jnp.broadcast_to(jnp.arange(UTTS, dtype=jnp.int32)[:, None], (UTTS, FRAMES))
    buffer = jnp.zeros((EXPERTS, UTTS, CAP, D), jnp.bfloat16)
    buffer = buffer.at[chosen_ids, utter, slot].add(jnp.where(sent[..., None], expert_in, jnp.zeros_like(expert_in)))

    def run_expert(item):
        block, index = item
        first = lax.dynamic_slice_in_dim(w_in, index * FF, FF, 1)
        second = lax.dynamic_slice_in_dim(w_out, index * FF, FF, 0)
        flat = block.reshape(UTTS * CAP, D)
        hidden = jax.nn.silu(jnp.dot(flat, first, preferred_element_type=jnp.float32)).astype(jnp.bfloat16)
        result = jnp.dot(hidden, second, preferred_element_type=jnp.float32).astype(jnp.bfloat16)
        return result.reshape(UTTS, CAP, D)
    results = lax.map(run_expert, (buffer, jnp.arange(EXPERTS, dtype=jnp.int32)))
    picked = results[chosen_ids, utter, slot].astype(jnp.float32) * sent[..., None].astype(jnp.float32)
    total = stream.astype(jnp.float32) + 0.5 * gate[..., None] * picked
    return (layer_norm(total) * final_gain).astype(jnp.bfloat16)
```

```python
import functools

import jax
import jax.numpy as jnp
from jax import lax
from jax.experimental import pallas as pl
from jax.experimental.pallas import tpu as pltpu
from jax.sharding import PartitionSpec as P

LANES = 128
ROWS = 8
BLOCK = 64
EPS = 1e-05
MIB = 1 << 20


def xor_route(block, axis, distance):
    count = lax.axis_size(axis)
    return lax.ppermute(block, axis, [(i, i ^ distance) for i in range(count)])


def exchange(block, axis, chips):
    count = lax.axis_size(axis)
    same_core = [list(range(core, count, 2)) for core in range(2)]
    blocks = block.reshape(chips, block.shape[0] // chips, block.shape[1])
    moved = lax.all_to_all(blocks, axis, split_axis=0, concat_axis=0, tiled=True, axis_index_groups=same_core)
    return moved.reshape(block.shape)


def silu(value):
    return value / (1.0 + jnp.exp(-value))


def normalise(values):
    mean = jnp.mean(values, axis=-1, keepdims=True)
    centred = values - mean
    variance = jnp.mean(centred * centred, axis=-1, keepdims=True)
    return centred * lax.rsqrt(variance + EPS)


def pre_kernel(cap, pitch, count_ref, frames_ref, ids_ref, taps_ref, stream_ref, expert_in_ref, slot_ref, *rest):
    *message_refs, padded, taps_by_row, conv = rest
    length, width = frames_ref.shape
    taps = taps_ref.shape[0]
    reach = taps // 2
    groups = width // LANES
    count = count_ref[0]

    for group in range(groups):
        lanes = slice(group * LANES, (group + 1) * LANES)
        taps_by_row[pl.ds(group, taps, stride=groups), :] = taps_ref[:, lanes]
    edge = jnp.zeros((reach * groups, LANES), jnp.float32)
    padded[: reach * groups, :] = edge
    padded[(reach + length) * groups :, :] = edge
    for start in range(0, length, BLOCK):
        values = frames_ref[start : start + BLOCK, :].astype(jnp.float32)
        position = start + lax.broadcasted_iota(jnp.int32, (BLOCK, 1), 0)
        normed = jnp.where(position < count, normalise(values), 0.0)
        for group in range(groups):
            lanes = slice(group * LANES, (group + 1) * LANES)
            padded[pl.ds((reach + start) * groups + group, BLOCK, stride=groups), :] = normed[:, lanes]

    def convolve(index, carry):
        base = pl.multiple_of(index * (ROWS * groups), ROWS * groups)
        window = [padded[pl.ds(base + step * groups, groups), :] for step in range(ROWS + taps - 1)]
        sums = [None] * ROWS
        for tap in range(taps):
            weight = taps_by_row[tap * groups : (tap + 1) * groups, :]
            for row in range(ROWS):
                term = weight * window[row + tap]
                sums[row] = term if tap == 0 else sums[row] + term
        for row in range(ROWS):
            conv[pl.ds(base + row * groups, groups), :] = sums[row]
        return carry

    lax.fori_loop(0, length // ROWS, convolve, 0)

    for start in range(0, length, BLOCK):
        rows = slice(start, start + BLOCK)
        mixed = jnp.concatenate(
            [conv[pl.ds(start * groups + group, BLOCK, stride=groups), :] for group in range(groups)], axis=1
        )
        stream = (frames_ref[rows, :].astype(jnp.float32) + silu(mixed)).astype(jnp.bfloat16)
        stream_ref[rows, :] = stream
        expert_in_ref[rows, :] = normalise(stream.astype(jnp.float32)).astype(jnp.bfloat16)

    chips = slot_ref.shape[0]
    ids = ids_ref[...]
    at = lax.broadcasted_iota(jnp.int32, (chips, length), 1)
    chosen = (ids == lax.broadcasted_iota(jnp.int32, (chips, length), 0)) & (at < count)
    earlier = lax.broadcasted_iota(jnp.int32, (length, length), 0) < lax.broadcasted_iota(
        jnp.int32, (length, length), 1
    )
    before = jnp.dot(
        chosen.astype(jnp.bfloat16), earlier.astype(jnp.bfloat16), preferred_element_type=jnp.float32
    )
    rank = jnp.sum(jnp.where(chosen, before, 0.0), axis=0, keepdims=True).astype(jnp.int32)
    sent = (at[:1] < count) & (rank < cap)
    slot = jnp.where(sent, ids * pitch + rank, -1)
    slot_ref[...] = jnp.broadcast_to(slot, slot_ref.shape)
    slots = chips * pitch
    placing = (slot == lax.broadcasted_iota(jnp.int32, (slots, length), 0)).astype(jnp.bfloat16)
    span = slots // len(message_refs)
    for start in range(0, width, 256):
        columns = slice(start, start + 256)
        placed = jnp.dot(placing, expert_in_ref[:, columns], preferred_element_type=jnp.float32)
        placed = placed.astype(jnp.bfloat16)
        for number, message in enumerate(message_refs):
            message[:, columns] = placed[number * span : (number + 1) * span, :]


def prepare(frames, count, ids, taps, chips, cap, pitch, messages):
    length, width = frames.shape
    groups = width // LANES
    reach = taps.shape[0] // 2
    whole = pl.BlockSpec(memory_space=pltpu.VMEM)
    span = chips * pitch // messages
    bf16 = jnp.bfloat16
    return pl.pallas_call(
        functools.partial(pre_kernel, cap, pitch),
        in_specs=[pl.BlockSpec(memory_space=pltpu.SMEM), whole, whole, whole],
        out_specs=[whole] * (3 + messages),
        out_shape=[
            jax.ShapeDtypeStruct((length, width), bf16),
            jax.ShapeDtypeStruct((length, width), bf16),
            jax.ShapeDtypeStruct((chips, length), jnp.int32),
        ]
        + [jax.ShapeDtypeStruct((span, width), bf16)] * messages,
        scratch_shapes=[
            pltpu.VMEM(((length + 2 * reach) * groups, LANES), jnp.float32),
            pltpu.VMEM((taps.shape[0] * groups, LANES), jnp.float32),
            pltpu.VMEM((length * groups, LANES), jnp.float32),
        ],
        compiler_params=pltpu.CompilerParams(vmem_limit_bytes=24 * MIB),
        cost_estimate=pl.CostEstimate(flops=4 * 10**8, bytes_accessed=4 * 10**6, transcendentals=0),
        name="prepare",
    )(count, frames, ids, taps)


def gate_kernel(pitch, count_ref, expert_in_ref, router_ref, ids_ref, slot_ref, gate_ref, picking_ref):
    length = expert_in_ref.shape[0]
    experts = router_ref.shape[1]
    slots = picking_ref.shape[1]
    logits = jnp.dot(expert_in_ref[...], router_ref[...], preferred_element_type=jnp.float32)
    ids = jnp.broadcast_to(ids_ref[...].astype(jnp.float32), (experts, length)).T
    position = lax.broadcasted_iota(jnp.int32, (length, experts), 0)
    column = lax.broadcasted_iota(jnp.int32, (length, experts), 1).astype(jnp.float32)
    chosen = (ids == column) & (position < count_ref[0])
    logit = jnp.sum(jnp.where(chosen, logits, 0.0), axis=1, keepdims=True)
    gate_ref[...] = 0.5 / (1.0 + jnp.exp(-logit))
    slot = slot_ref[...].astype(jnp.float32).T[:, :1].astype(jnp.int32)
    picking_ref[...] = (slot == lax.broadcasted_iota(jnp.int32, (length, slots), 1)).astype(jnp.bfloat16)


def gate_and_picking(count, expert_in, router, ids, slot, pitch):
    length = expert_in.shape[0]
    slots = slot.shape[0] * pitch
    whole = pl.BlockSpec(memory_space=pltpu.VMEM)
    return pl.pallas_call(
        functools.partial(gate_kernel, pitch),
        in_specs=[pl.BlockSpec(memory_space=pltpu.SMEM)] + [whole] * 4,
        out_specs=[whole] * 2,
        out_shape=[
            jax.ShapeDtypeStruct((length, 1), jnp.float32),
            jax.ShapeDtypeStruct((length, slots), jnp.bfloat16),
        ],
        compiler_params=pltpu.CompilerParams(vmem_limit_bytes=12 * MIB),
        name="gate",
    )(count, expert_in, router, ids, slot)


def expert_kernel(parts, tile, *refs):
    inputs, (in_a, in_b, out_a, out_b) = refs[:parts], refs[parts : parts + 4]
    outputs, (rows, total) = refs[parts + 4 : 2 * parts + 4], refs[2 * parts + 4 :]
    span = inputs[0].shape[0]
    for number, part in enumerate(inputs):
        rows[number * span : (number + 1) * span, :] = part[...]
    values = rows[...]
    hidden = in_a.shape[1]

    def step(index, carry):
        units = pl.ds(pl.multiple_of(index * tile, tile), tile)
        result = None
        for first, second in ((in_a, out_a), (in_b, out_b)):
            mid = silu(jnp.dot(values, first[:, units], preferred_element_type=jnp.float32)).astype(jnp.bfloat16)
            term = jnp.dot(mid, second[units, :], preferred_element_type=jnp.float32)
            result = term if result is None else result + term

        @pl.when(index == 0)
        def _():
            total[...] = result

        @pl.when(index > 0)
        def _():
            total[...] += result

        return carry

    lax.fori_loop(0, hidden // tile, step, 0)
    for number, part in enumerate(outputs):
        part[...] = total[number * span : (number + 1) * span, :].astype(jnp.bfloat16)


def run_expert(parts, weights):
    span, width = parts[0].shape
    whole = pl.BlockSpec(memory_space=pltpu.VMEM)
    count = len(parts)
    hidden = weights[0].shape[1]
    return pl.pallas_call(
        functools.partial(expert_kernel, count, min(1024, hidden)),
        in_specs=[whole] * (count + 4),
        out_specs=[whole] * count,
        out_shape=[jax.ShapeDtypeStruct((span, width), jnp.bfloat16)] * count,
        scratch_shapes=[
            pltpu.VMEM((span * count, width), jnp.bfloat16),
            pltpu.VMEM((span * count, width), jnp.float32),
        ],
        compiler_params=pltpu.CompilerParams(vmem_limit_bytes=36 * MIB),
        cost_estimate=pl.CostEstimate(
            flops=8 * span * count * width * hidden, bytes_accessed=8 * width * hidden, transcendentals=0
        ),
        name="expert",
    )(*parts, *weights)


def final_kernel(parts, stream_ref, gate_ref, picking_ref, gain_ref, *refs):
    inputs, out_ref, results = refs[:parts], refs[parts], refs[parts + 1]
    span = inputs[0].shape[0]
    for number, part in enumerate(inputs):
        results[number * span : (number + 1) * span, :] = part[...]
    picked = jnp.dot(picking_ref[...], results[...], preferred_element_type=jnp.float32)
    total = stream_ref[...].astype(jnp.float32) + gate_ref[...] * picked
    out_ref[...] = (normalise(total) * gain_ref[...]).astype(jnp.bfloat16)


def finish(stream, gate, picking, gain, parts):
    length, width = stream.shape
    whole = pl.BlockSpec(memory_space=pltpu.VMEM)
    span = parts[0].shape[0]
    return pl.pallas_call(
        functools.partial(final_kernel, len(parts)),
        in_specs=[whole] * (4 + len(parts)),
        out_specs=whole,
        out_shape=jax.ShapeDtypeStruct((length, width), jnp.bfloat16),
        scratch_shapes=[pltpu.VMEM((span * len(parts), width), jnp.bfloat16)],
        compiler_params=pltpu.CompilerParams(vmem_limit_bytes=24 * MIB),
        name="finish",
    )(stream, gate, picking, gain, *parts)


def on_device(frames, frame_counts, expert_ids, conv_kernel, router, w_in, w_out, final_gain):
    _, length, width = frames.shape
    n_dev = lax.axis_size("expert")
    chips = n_dev // 2
    cap = 2 * ((5 * length + 8 * chips - 1) // (8 * chips))
    me = lax.axis_index("expert") // 2
    other_in = xor_route(w_in, "expert", 1)
    other_out = xor_route(w_out, "expert", 1)
    weights = (w_in, other_in, w_out, other_out)
    ids = expert_ids.reshape(1, length)
    gain = final_gain.reshape(1, width)

    if chips <= 8:
        pitch = -(-cap // 16) * 16
        stream, expert_in, slot, *messages = prepare(
            frames[0], frame_counts, ids ^ me, conv_kernel, chips, cap, pitch, chips
        )
        gate, picking = gate_and_picking(frame_counts, expert_in, router, ids, slot, pitch)
        far = [d for d in range(1, chips) if d >= chips // 2]
        near = [d for d in range(1, chips) if d < chips // 2]
        half = max(1, len(far) // 2)
        arrived = {0: messages[0]}
        for d in far + near:
            arrived[d] = xor_route(messages[d], "expert", 2 * d)
        results = {}
        for batch in (far[:half], far[half:], [0] + near):
            if batch:
                for d, part in zip(batch, run_expert([arrived[d] for d in batch], weights)):
                    results[d] = part if d == 0 else xor_route(part, "expert", 2 * d)
        parts = [results[d] for d in range(chips)]
    else:
        stream, expert_in, slot, message = prepare(frames[0], frame_counts, ids, conv_kernel, chips, cap, cap, 1)
        gate, picking = gate_and_picking(frame_counts, expert_in, router, ids, slot, cap)
        (result,) = run_expert([exchange(message, "expert", chips)], weights)
        parts = [exchange(result, "expert", chips)]
    return finish(stream, gate, picking, gain, parts).reshape(1, length, width)


def solution(mesh):
    return jax.shard_map(
        on_device,
        mesh=mesh,
        in_specs=(
            P(("groups", "expert"), None, None),
            P(("groups", "expert")),
            P(("groups", "expert"), None, None),
            P(),
            P(),
            P(None, "expert"),
            P("expert", None),
            P(),
        ),
        out_specs=P(("groups", "expert"), None, None),
        check_vma=False,
    )
```

```python
import functools

import jax
import jax.numpy as jnp
from jax import lax
from jax.experimental import pallas as pl
from jax.experimental.pallas import tpu as pltpu
from jax.sharding import PartitionSpec as P

LANES = 128
ROWS = 8
BLOCK = 64
EPS = 1e-05
SMALL = pl.CostEstimate(flops=1, bytes_accessed=1, transcendentals=0)
MIB = 1 << 20


def xor_route(block, axis, distance):
    count = lax.axis_size(axis)
    return lax.ppermute(block, axis, [(i, i ^ distance) for i in range(count)])


def after(values, earlier):
    return lax.optimization_barrier((values, earlier))[0]


def exchange(block, axis, chips):
    count = lax.axis_size(axis)
    same_core = [list(range(core, count, 2)) for core in range(2)]
    blocks = block.reshape(chips, block.shape[0] // chips, block.shape[1])
    moved = lax.all_to_all(blocks, axis, split_axis=0, concat_axis=0, tiled=True, axis_index_groups=same_core)
    return moved.reshape(block.shape)


def in_hbm(array):
    return pltpu.with_memory_space_constraint(array, pltpu.HBM)


def silu(value):
    return value / (1.0 + jnp.exp(-value))


def normalise(values):
    mean = jnp.mean(values, axis=-1, keepdims=True)
    centred = values - mean
    variance = jnp.mean(centred * centred, axis=-1, keepdims=True)
    return centred * lax.rsqrt(variance + EPS)


def pre_kernel(cap, pitch, count_ref, me_ref, frames_hbm, ids_ref, taps_hbm, in_hbm, out_hbm, *rest):
    in_ref, out_ref, stream_ref, expert_in_ref, slot_ref, *rest = rest
    *message_refs, frames_ref, taps_ref, padded, taps_by_row, conv, frame_sems, taps_sem, weight_sems = rest
    length, width = frames_ref.shape
    taps = taps_ref.shape[0]
    reach = taps // 2
    groups = width // LANES
    count = count_ref[0]

    frame_copies = [
        pltpu.make_async_copy(
            frames_hbm.at[0, pl.ds(start, BLOCK), :], frames_ref.at[pl.ds(start, BLOCK), :], frame_sems.at[number]
        )
        for number, start in enumerate(range(0, length, BLOCK))
    ]
    taps_copy = pltpu.make_async_copy(taps_hbm, taps_ref, taps_sem)
    for copy in frame_copies:
        copy.start()
    taps_copy.start()
    weight_copies = [
        pltpu.make_async_copy(in_hbm, in_ref, weight_sems.at[0]),
        pltpu.make_async_copy(out_hbm, out_ref, weight_sems.at[1]),
    ]
    for copy in weight_copies:
        copy.start()

    edge = jnp.zeros((reach * groups, LANES), jnp.float32)
    padded[: reach * groups, :] = edge
    padded[(reach + length) * groups :, :] = edge
    for number, start in enumerate(range(0, length, BLOCK)):
        frame_copies[number].wait()
        values = frames_ref[start : start + BLOCK, :].astype(jnp.float32)
        position = start + lax.broadcasted_iota(jnp.int32, (BLOCK, 1), 0)
        normed = jnp.where(position < count, normalise(values), 0.0)
        for group in range(groups):
            lanes = slice(group * LANES, (group + 1) * LANES)
            padded[pl.ds((reach + start) * groups + group, BLOCK, stride=groups), :] = normed[:, lanes]

    taps_copy.wait()
    for group in range(groups):
        lanes = slice(group * LANES, (group + 1) * LANES)
        taps_by_row[pl.ds(group, taps, stride=groups), :] = taps_ref[:, lanes]

    def convolve(index, carry):
        base = pl.multiple_of(index * (ROWS * groups), ROWS * groups)
        window = [padded[pl.ds(base + step * groups, groups), :] for step in range(ROWS + taps - 1)]
        sums = [None] * ROWS
        for tap in range(taps):
            weight = taps_by_row[tap * groups : (tap + 1) * groups, :]
            for row in range(ROWS):
                term = weight * window[row + tap]
                sums[row] = term if tap == 0 else sums[row] + term
        for row in range(ROWS):
            conv[pl.ds(base + row * groups, groups), :] = sums[row]
        return carry

    lax.fori_loop(0, length // ROWS, convolve, 0)

    for start in range(0, length, BLOCK):
        rows = slice(start, start + BLOCK)
        mixed = jnp.concatenate(
            [conv[pl.ds(start * groups + group, BLOCK, stride=groups), :] for group in range(groups)], axis=1
        )
        stream = (frames_ref[rows, :].astype(jnp.float32) + silu(mixed)).astype(jnp.bfloat16)
        stream_ref[rows, :] = stream
        expert_in_ref[rows, :] = normalise(stream.astype(jnp.float32)).astype(jnp.bfloat16)

    chips = slot_ref.shape[0]
    ids = ids_ref[...] ^ me_ref[0]
    at = lax.broadcasted_iota(jnp.int32, (chips, length), 1)
    chosen = (ids == lax.broadcasted_iota(jnp.int32, (chips, length), 0)) & (at < count)
    earlier = lax.broadcasted_iota(jnp.int32, (length, length), 0) < lax.broadcasted_iota(
        jnp.int32, (length, length), 1
    )
    before = jnp.dot(
        chosen.astype(jnp.bfloat16), earlier.astype(jnp.bfloat16), preferred_element_type=jnp.float32
    )
    rank = jnp.sum(jnp.where(chosen, before, 0.0), axis=0, keepdims=True).astype(jnp.int32)
    sent = (at[:1] < count) & (rank < cap)
    slot = jnp.where(sent, ids * pitch + rank, -1)
    slot_ref[...] = jnp.broadcast_to(slot, slot_ref.shape)
    slots = chips * pitch
    placing = (slot == lax.broadcasted_iota(jnp.int32, (slots, length), 0)).astype(jnp.bfloat16)
    span = slots // len(message_refs)
    for start in range(0, width, 256):
        columns = slice(start, start + 256)
        placed = jnp.dot(placing, expert_in_ref[:, columns], preferred_element_type=jnp.float32)
        placed = placed.astype(jnp.bfloat16)
        for number, message in enumerate(message_refs):
            message[:, columns] = placed[number * span : (number + 1) * span, :]
    for copy in weight_copies:
        copy.wait()


def prepare(frames, count, me, ids, taps, w_in, w_out, chips, cap, pitch, messages):
    _, length, width = frames.shape
    groups = width // LANES
    reach = taps.shape[0] // 2
    whole = pl.BlockSpec(memory_space=pltpu.VMEM)
    anywhere = pl.BlockSpec(memory_space=pl.ANY)
    span = chips * pitch // messages
    bf16 = jnp.bfloat16
    return pl.pallas_call(
        functools.partial(pre_kernel, cap, pitch),
        in_specs=[pl.BlockSpec(memory_space=pltpu.SMEM)] * 2 + [anywhere, whole] + [anywhere] * 3,
        out_specs=[whole] * (5 + messages),
        out_shape=[
            pltpu.VMEM(w_in.shape, bf16),
            pltpu.VMEM(w_out.shape, bf16),
            jax.ShapeDtypeStruct((length, width), bf16),
            jax.ShapeDtypeStruct((length, width), bf16),
            jax.ShapeDtypeStruct((chips, length), jnp.int32),
        ]
        + [jax.ShapeDtypeStruct((span, width), bf16)] * messages,
        scratch_shapes=[
            pltpu.VMEM((length, width), bf16),
            pltpu.VMEM(taps.shape, jnp.float32),
            pltpu.VMEM(((length + 2 * reach) * groups, LANES), jnp.float32),
            pltpu.VMEM((taps.shape[0] * groups, LANES), jnp.float32),
            pltpu.VMEM((length * groups, LANES), jnp.float32),
            pltpu.SemaphoreType.DMA((length // BLOCK,)),
            pltpu.SemaphoreType.DMA,
            pltpu.SemaphoreType.DMA((2,)),
        ],
        compiler_params=pltpu.CompilerParams(vmem_limit_bytes=24 * MIB),
        cost_estimate=SMALL,
        name="prepare",
    )(count, me, in_hbm(frames), ids, in_hbm(taps), in_hbm(w_in), in_hbm(w_out))


def load_kernel(count, *refs):
    sources, targets, sems = refs[:count], refs[count : 2 * count], refs[2 * count]
    copies = [pltpu.make_async_copy(a, b, sems.at[i]) for i, (a, b) in enumerate(zip(sources, targets))]
    for copy in copies:
        copy.start()
    for copy in copies:
        copy.wait()


def load(*arrays):
    count = len(arrays)
    return pl.pallas_call(
        functools.partial(load_kernel, count),
        in_specs=[pl.BlockSpec(memory_space=pl.ANY)] * count,
        out_specs=[pl.BlockSpec(memory_space=pltpu.VMEM)] * count,
        out_shape=[pltpu.VMEM(array.shape, array.dtype) for array in arrays],
        scratch_shapes=[pltpu.SemaphoreType.DMA((count,))],
        compiler_params=pltpu.CompilerParams(vmem_limit_bytes=4 * MIB),
        cost_estimate=SMALL,
        name="load",
    )(*[in_hbm(array) for array in arrays])


def gate_kernel(pitch, count_ref, expert_in_ref, router_ref, ids_ref, slot_ref, gate_ref, picking_ref):
    length = expert_in_ref.shape[0]
    experts = router_ref.shape[1]
    slots = picking_ref.shape[1]
    logits = jnp.dot(expert_in_ref[...], router_ref[...], preferred_element_type=jnp.float32)
    ids = jnp.broadcast_to(ids_ref[...].astype(jnp.float32), (experts, length)).T
    position = lax.broadcasted_iota(jnp.int32, (length, experts), 0)
    column = lax.broadcasted_iota(jnp.int32, (length, experts), 1).astype(jnp.float32)
    chosen = (ids == column) & (position < count_ref[0])
    logit = jnp.sum(jnp.where(chosen, logits, 0.0), axis=1, keepdims=True)
    gate_ref[...] = 0.5 / (1.0 + jnp.exp(-logit))
    slot = slot_ref[...].astype(jnp.float32).T[:, :1].astype(jnp.int32)
    picking_ref[...] = (slot == lax.broadcasted_iota(jnp.int32, (length, slots), 1)).astype(jnp.bfloat16)


def gate_and_picking(count, expert_in, router, ids, slot, pitch):
    length = expert_in.shape[0]
    slots = slot.shape[0] * pitch
    whole = pl.BlockSpec(memory_space=pltpu.VMEM)
    return pl.pallas_call(
        functools.partial(gate_kernel, pitch),
        in_specs=[pl.BlockSpec(memory_space=pltpu.SMEM)] + [whole] * 4,
        out_specs=[whole] * 2,
        out_shape=[
            jax.ShapeDtypeStruct((length, 1), jnp.float32),
            jax.ShapeDtypeStruct((length, slots), jnp.bfloat16),
        ],
        compiler_params=pltpu.CompilerParams(vmem_limit_bytes=12 * MIB),
        cost_estimate=SMALL,
        name="gate",
    )(count, expert_in, router, ids, slot)


def expert_kernel(parts, tile, *refs):
    inputs, (in_a, in_b, out_a, out_b) = refs[:parts], refs[parts : parts + 4]
    outputs, (rows, total) = refs[parts + 4 : 2 * parts + 4], refs[2 * parts + 4 :]
    span = inputs[0].shape[0]
    for number, part in enumerate(inputs):
        rows[number * span : (number + 1) * span, :] = part[...]
    values = rows[...]
    hidden = in_a.shape[1]

    def step(index, carry):
        units = pl.ds(pl.multiple_of(index * tile, tile), tile)
        result = None
        for first, second in ((in_a, out_a), (in_b, out_b)):
            mid = silu(jnp.dot(values, first[:, units], preferred_element_type=jnp.float32)).astype(jnp.bfloat16)
            term = jnp.dot(mid, second[units, :], preferred_element_type=jnp.float32)
            result = term if result is None else result + term

        @pl.when(index == 0)
        def _():
            total[...] = result

        @pl.when(index > 0)
        def _():
            total[...] += result

        return carry

    lax.fori_loop(0, hidden // tile, step, 0)
    for number, part in enumerate(outputs):
        part[...] = total[number * span : (number + 1) * span, :].astype(jnp.bfloat16)


def run_expert(parts, weights):
    span, width = parts[0].shape
    whole = pl.BlockSpec(memory_space=pltpu.VMEM)
    count = len(parts)
    hidden = weights[0].shape[1]
    return pl.pallas_call(
        functools.partial(expert_kernel, count, min(1024, hidden)),
        in_specs=[whole] * (count + 4),
        out_specs=[whole] * count,
        out_shape=[jax.ShapeDtypeStruct((span, width), jnp.bfloat16)] * count,
        scratch_shapes=[
            pltpu.VMEM((span * count, width), jnp.bfloat16),
            pltpu.VMEM((span * count, width), jnp.float32),
        ],
        compiler_params=pltpu.CompilerParams(vmem_limit_bytes=16 * MIB),
        cost_estimate=SMALL,
        name="expert",
    )(*parts, *weights)


def add_kernel(parts, order, picking_ref, so_far_ref, gate_ref, *refs):
    inputs, out_ref, results = refs[:parts], refs[parts], refs[parts + 1]
    span = inputs[0].shape[0]
    places = []
    for number, (part, at) in enumerate(zip(inputs, order)):
        results[number * span : (number + 1) * span, :] = part[...]
        places.append(picking_ref[:, at * span : (at + 1) * span])
    picking = jnp.concatenate(places, axis=1) if parts > 1 else places[0]
    picked = jnp.dot(picking, results[...], preferred_element_type=jnp.float32)
    out_ref[...] = so_far_ref[...].astype(jnp.float32) + gate_ref[...] * picked


def close_kernel(parts, order, picking_ref, so_far_ref, gate_ref, gain_ref, *refs):
    *refs, out_ref, results, total = refs
    add_kernel(parts, order, picking_ref, so_far_ref, gate_ref, *refs, total, results)
    out_ref[...] = (normalise(total[...]) * gain_ref[...]).astype(jnp.bfloat16)


def add_results(so_far, gate, picking, parts, gain=None):
    length, width = so_far.shape
    whole = pl.BlockSpec(memory_space=pltpu.VMEM)
    order, values = tuple(parts), [parts[at] for at in parts]
    span = values[0].shape[0]
    scratch = [pltpu.VMEM((span * len(parts), width), jnp.bfloat16)]
    last = gain is not None
    if last:
        scratch.append(pltpu.VMEM((length, width), jnp.float32))
    return pl.pallas_call(
        functools.partial(close_kernel if last else add_kernel, len(parts), order),
        in_specs=[whole] * (3 + last + len(parts)),
        out_specs=whole,
        out_shape=jax.ShapeDtypeStruct((length, width), jnp.bfloat16 if last else jnp.float32),
        scratch_shapes=scratch,
        compiler_params=pltpu.CompilerParams(vmem_limit_bytes=24 * MIB),
        cost_estimate=SMALL,
        name="finish" if last else "add",
    )(picking, so_far, gate, *([gain] if last else []), *values)


def on_device(frames, frame_counts, expert_ids, conv_kernel, router, w_in, w_out, final_gain):
    _, length, width = frames.shape
    n_dev = lax.axis_size("expert")
    chips = n_dev // 2
    cap = 2 * ((5 * length + 8 * chips - 1) // (8 * chips))
    chip = (lax.axis_index("expert") // 2).astype(jnp.int32).reshape(1)
    other_in = xor_route(w_in, "expert", 1)
    other_out = xor_route(w_out, "expert", 1)
    ids = expert_ids.reshape(1, length)
    gain = final_gain.reshape(1, width)

    if chips <= 8:
        pitch = -(-cap // 16) * 16
        own_in, own_out, stream, expert_in, slot, *messages = prepare(
            frames, frame_counts, chip, ids, conv_kernel, w_in, w_out, chips, cap, pitch, chips
        )
        send = lambda part, d: xor_route(part, "expert", 2 * d)
        far = [d for d in range(1, chips) if d >= chips // 2]
        near = [d for d in range(1, chips) if d < chips // 2]
        half = max(1, len(far) // 2)
        first, second = far[:half], far[half:]
        arrived = {d: send(messages[d], d) for d in far}
        other_in, other_out = load(other_in, other_out)
        weights = (own_in, other_in, own_out, other_out)
        results = {}
        first_out = run_expert([arrived[d] for d in first], weights)
        for d, part in zip(first, first_out):
            results[d] = send(part, d)
        gate, picking = gate_and_picking(frame_counts, expert_in, router, ids, slot, pitch)
        held = after([messages[d] for d in near], [arrived[d] for d in first])
        for d, part in zip(near, held):
            arrived[d] = send(part, d)
        second_out = run_expert(after([arrived[d] for d in second], first_out), weights)
        for d, part in zip(second, second_out):
            results[d] = send(part, d)
        close = run_expert([messages[0]] + after([arrived[d] for d in near], second_out), weights)
        for d, part in zip([0] + near, close):
            results[d] = part if d == 0 else send(part, d)
        total = add_results(stream, gate, picking, {d: results[d] for d in first})
        output = add_results(total, gate, picking, {d: results[d] for d in second + [0] + near}, gain)
    else:
        home = jnp.zeros((1,), jnp.int32)
        own_in, own_out, stream, expert_in, slot, message = prepare(
            frames, frame_counts, home, ids, conv_kernel, w_in, w_out, chips, cap, cap, 1
        )
        gate, picking = gate_and_picking(frame_counts, expert_in, router, ids, slot, cap)
        other_in, other_out = load(other_in, other_out)
        (result,) = run_expert([exchange(message, "expert", chips)], (own_in, other_in, own_out, other_out))
        output = add_results(stream, gate, picking, {0: exchange(result, "expert", chips)}, gain)
    return output.reshape(1, length, width)


def solution(mesh):
    return jax.shard_map(
        on_device,
        mesh=mesh,
        in_specs=(
            P(("groups", "expert"), None, None),
            P(("groups", "expert")),
            P(("groups", "expert"), None, None),
            P(),
            P(),
            P(None, "expert"),
            P("expert", None),
            P(),
        ),
        out_specs=P(("groups", "expert"), None, None),
        check_vma=False,
    )
```

```python
import functools

import jax
import jax.numpy as jnp
from jax import lax
from jax.experimental import pallas as pl
from jax.experimental.pallas import tpu as pltpu
from jax.sharding import PartitionSpec as P

LANES = 128
ROWS = 8
BLOCK = 64
EPS = 1e-05
SMALL = pl.CostEstimate(flops=1, bytes_accessed=1, transcendentals=0)
MIB = 1 << 20


def xor_route(block, axis, distance):
    count = lax.axis_size(axis)
    return lax.ppermute(block, axis, [(i, i ^ distance) for i in range(count)])


def after(values, earlier):
    return lax.optimization_barrier((values, earlier))[0]


def exchange(block, axis, chips):
    count = lax.axis_size(axis)
    same_core = [list(range(core, count, 2)) for core in range(2)]
    blocks = block.reshape(chips, block.shape[0] // chips, block.shape[1])
    moved = lax.all_to_all(blocks, axis, split_axis=0, concat_axis=0, tiled=True, axis_index_groups=same_core)
    return moved.reshape(block.shape)


def in_hbm(array):
    return pltpu.with_memory_space_constraint(array, pltpu.HBM)


def silu(value):
    return 0.5 * value * (1.0 + jnp.tanh(0.5 * value))


def normalise(values):
    mean = jnp.mean(values, axis=-1, keepdims=True)
    centred = values - mean
    variance = jnp.mean(centred * centred, axis=-1, keepdims=True)
    return centred * lax.rsqrt(variance + EPS)


def pre_kernel(cap, pitch, count_ref, me_ref, frames_hbm, ids_hbm, taps_hbm, in_hbm, out_hbm, *rest):
    in_ref, out_ref, stream_ref, expert_in_ref, slot_ref, *rest = rest
    *message_refs, frames_ref, taps_ref, ids_ref, padded, conv, frame_sems, taps_sem, ids_sem, weight_sems = rest
    length, width = frames_ref.shape
    taps = taps_ref.shape[0]
    reach = taps // 2
    groups = width // LANES
    count = count_ref[0]

    frame_copies = [
        pltpu.make_async_copy(
            frames_hbm.at[0, pl.ds(start, BLOCK), :], frames_ref.at[pl.ds(start, BLOCK), :], frame_sems.at[number]
        )
        for number, start in enumerate(range(0, length, BLOCK))
    ]
    taps_copy = pltpu.make_async_copy(taps_hbm, taps_ref, taps_sem)
    for copy in frame_copies:
        copy.start()
    taps_copy.start()
    ids_copy = pltpu.make_async_copy(ids_hbm, ids_ref, ids_sem)
    ids_copy.start()
    weight_copies = [
        pltpu.make_async_copy(in_hbm, in_ref, weight_sems.at[0]),
        pltpu.make_async_copy(out_hbm, out_ref, weight_sems.at[1]),
    ]
    lead = padded.shape[1] - length - reach
    padded[:, :lead, :] = jnp.zeros((groups, lead, LANES), jnp.float32)
    padded[:, lead + length :, :] = jnp.zeros((groups, reach, LANES), jnp.float32)
    for number, start in enumerate(range(0, length, BLOCK)):
        frame_copies[number].wait()
        values = frames_ref[start : start + BLOCK, :].astype(jnp.float32)
        position = start + lax.broadcasted_iota(jnp.int32, (BLOCK, 1), 0)
        normed = jnp.where(position < count, normalise(values), 0.0)
        for group in range(groups):
            padded[group, lead + start : lead + start + BLOCK, :] = normed[:, group * LANES : (group + 1) * LANES]

    for copy in weight_copies:
        copy.start()
    taps_copy.wait()

    def convolve(index, carry):
        group = lax.rem(index, groups)
        start = pl.multiple_of(lax.div(index, groups) * BLOCK, BLOCK)
        lanes = pl.ds(pl.multiple_of(group * LANES, LANES), LANES)
        total = None
        for tap in range(taps):
            term = taps_ref[pl.ds(tap, 1), lanes] * padded[group, pl.ds(start + (lead - reach + tap), BLOCK), :]
            total = term if tap == 0 else total + term
        conv[pl.ds(start, BLOCK), lanes] = total
        return carry

    lax.fori_loop(0, groups * (length // BLOCK), convolve, 0)

    for start in range(0, length, BLOCK):
        rows = slice(start, start + BLOCK)
        stream = (frames_ref[rows, :].astype(jnp.float32) + silu(conv[rows, :])).astype(jnp.bfloat16)
        stream_ref[rows, :] = stream
        expert_in_ref[rows, :] = normalise(stream.astype(jnp.float32)).astype(jnp.bfloat16)

    chips = slot_ref.shape[0]
    ids_copy.wait()
    ids = ids_ref[...] ^ me_ref[0]
    at = lax.broadcasted_iota(jnp.int32, (chips, length), 1)
    chosen = (ids == lax.broadcasted_iota(jnp.int32, (chips, length), 0)) & (at < count)
    earlier = lax.broadcasted_iota(jnp.int32, (length, length), 0) < lax.broadcasted_iota(
        jnp.int32, (length, length), 1
    )
    before = jnp.dot(
        chosen.astype(jnp.bfloat16), earlier.astype(jnp.bfloat16), preferred_element_type=jnp.float32
    )
    rank = jnp.sum(jnp.where(chosen, before, 0.0), axis=0, keepdims=True).astype(jnp.int32)
    sent = (at[:1] < count) & (rank < cap)
    slot = jnp.where(sent, ids * pitch + rank, -1)
    slot_ref[...] = jnp.broadcast_to(slot, slot_ref.shape)
    slots = chips * pitch
    placing = (slot == lax.broadcasted_iota(jnp.int32, (slots, length), 0)).astype(jnp.bfloat16)
    span = slots // len(message_refs)
    for start in range(0, width, 256):
        columns = slice(start, start + 256)
        placed = jnp.dot(placing, expert_in_ref[:, columns], preferred_element_type=jnp.float32)
        placed = placed.astype(jnp.bfloat16)
        for number, message in enumerate(message_refs):
            message[:, columns] = placed[number * span : (number + 1) * span, :]
    for copy in weight_copies:
        copy.wait()


def prepare(frames, count, me, ids, taps, w_in, w_out, chips, cap, pitch, messages):
    _, length, width = frames.shape
    groups = width // LANES
    reach = taps.shape[0] // 2
    whole = pl.BlockSpec(memory_space=pltpu.VMEM)
    anywhere = pl.BlockSpec(memory_space=pl.ANY)
    span = chips * pitch // messages
    bf16 = jnp.bfloat16
    return pl.pallas_call(
        functools.partial(pre_kernel, cap, pitch),
        in_specs=[pl.BlockSpec(memory_space=pltpu.SMEM)] * 2 + [anywhere] * 5,
        out_specs=[whole] * (5 + messages),
        out_shape=[
            pltpu.VMEM(w_in.shape, bf16),
            pltpu.VMEM(w_out.shape, bf16),
            jax.ShapeDtypeStruct((length, width), bf16),
            jax.ShapeDtypeStruct((length, width), bf16),
            jax.ShapeDtypeStruct((chips, length), jnp.int32),
        ]
        + [jax.ShapeDtypeStruct((span, width), bf16)] * messages,
        scratch_shapes=[
            pltpu.VMEM((length, width), bf16),
            pltpu.VMEM(taps.shape, jnp.float32),
            pltpu.VMEM(ids.shape, jnp.int32),
            pltpu.VMEM((groups, -(-reach // 8) * 8 + length + reach, LANES), jnp.float32),
            pltpu.VMEM((length, width), jnp.float32),
            pltpu.SemaphoreType.DMA((length // BLOCK,)),
            pltpu.SemaphoreType.DMA,
            pltpu.SemaphoreType.DMA,
            pltpu.SemaphoreType.DMA((2,)),
        ],
        compiler_params=pltpu.CompilerParams(vmem_limit_bytes=12 * MIB),
        cost_estimate=SMALL,
        name="prepare",
    )(count, me, in_hbm(frames), in_hbm(ids), in_hbm(taps), in_hbm(w_in), in_hbm(w_out))


def load_kernel(count, *refs):
    sources, targets, sems = refs[:count], refs[count : 2 * count], refs[2 * count]
    copies = [pltpu.make_async_copy(a, b, sems.at[i]) for i, (a, b) in enumerate(zip(sources, targets))]
    for copy in copies:
        copy.start()
    for copy in copies:
        copy.wait()


def load(*arrays):
    count = len(arrays)
    return pl.pallas_call(
        functools.partial(load_kernel, count),
        in_specs=[pl.BlockSpec(memory_space=pl.ANY)] * count,
        out_specs=[pl.BlockSpec(memory_space=pltpu.VMEM)] * count,
        out_shape=[pltpu.VMEM(array.shape, array.dtype) for array in arrays],
        scratch_shapes=[pltpu.SemaphoreType.DMA((count,))],
        compiler_params=pltpu.CompilerParams(vmem_limit_bytes=4 * MIB),
        cost_estimate=SMALL,
        name="load",
    )(*[in_hbm(array) for array in arrays])


def gate_kernel(pitch, count_ref, expert_in_ref, router_ref, ids_ref, slot_ref, gate_ref, picking_ref):
    length = expert_in_ref.shape[0]
    experts = router_ref.shape[0]
    slots = picking_ref.shape[1]
    logits = lax.dot_general(
        expert_in_ref[...], router_ref[...], (((1,), (1,)), ((), ())), preferred_element_type=jnp.float32
    )
    ids = jnp.broadcast_to(ids_ref[...].astype(jnp.float32), (experts, length)).T
    position = lax.broadcasted_iota(jnp.int32, (length, experts), 0)
    column = lax.broadcasted_iota(jnp.int32, (length, experts), 1).astype(jnp.float32)
    chosen = (ids == column) & (position < count_ref[0])
    logit = jnp.sum(jnp.where(chosen, logits, 0.0), axis=1, keepdims=True)
    gate_ref[...] = 0.5 / (1.0 + jnp.exp(-logit))
    slot = slot_ref[...].astype(jnp.float32).T[:, :1].astype(jnp.int32)
    picking_ref[...] = (slot == lax.broadcasted_iota(jnp.int32, (length, slots), 1)).astype(jnp.bfloat16)


def gate_and_picking(count, expert_in, router, ids, slot, pitch):
    length = expert_in.shape[0]
    slots = slot.shape[0] * pitch
    whole = pl.BlockSpec(memory_space=pltpu.VMEM)
    return pl.pallas_call(
        functools.partial(gate_kernel, pitch),
        in_specs=[pl.BlockSpec(memory_space=pltpu.SMEM)] + [whole] * 4,
        out_specs=[whole] * 2,
        out_shape=[
            jax.ShapeDtypeStruct((length, 1), jnp.float32),
            jax.ShapeDtypeStruct((length, slots), jnp.bfloat16),
        ],
        compiler_params=pltpu.CompilerParams(vmem_limit_bytes=12 * MIB),
        cost_estimate=SMALL,
        name="gate",
    )(count, expert_in, router.T, ids, slot)


def expert_kernel(parts, tile, *refs):
    inputs, (in_a, in_b, out_a, out_b) = refs[:parts], refs[parts : parts + 4]
    outputs, (rows, total) = refs[parts + 4 : 2 * parts + 4], refs[2 * parts + 4 :]
    span = inputs[0].shape[0]
    for number, part in enumerate(inputs):
        rows[number * span : (number + 1) * span, :] = part[...]
    values = rows[...]
    hidden = in_a.shape[1]

    def step(index, carry):
        units = pl.ds(pl.multiple_of(index * tile, tile), tile)
        result = None
        for first, second in ((in_a, out_a), (in_b, out_b)):
            mid = silu(jnp.dot(values, first[:, units], preferred_element_type=jnp.float32)).astype(jnp.bfloat16)
            term = jnp.dot(mid, second[units, :], preferred_element_type=jnp.float32)
            result = term if result is None else result + term

        @pl.when(index == 0)
        def _():
            total[...] = result

        @pl.when(index > 0)
        def _():
            total[...] += result

        return carry

    lax.fori_loop(0, hidden // tile, step, 0)
    for number, part in enumerate(outputs):
        part[...] = total[number * span : (number + 1) * span, :].astype(jnp.bfloat16)


def run_expert(parts, weights):
    span, width = parts[0].shape
    whole = pl.BlockSpec(memory_space=pltpu.VMEM)
    count = len(parts)
    hidden = weights[0].shape[1]
    return pl.pallas_call(
        functools.partial(expert_kernel, count, min(1024, hidden)),
        in_specs=[whole] * (count + 4),
        out_specs=[whole] * count,
        out_shape=[jax.ShapeDtypeStruct((span, width), jnp.bfloat16)] * count,
        scratch_shapes=[
            pltpu.VMEM((span * count, width), jnp.bfloat16),
            pltpu.VMEM((span * count, width), jnp.float32),
        ],
        compiler_params=pltpu.CompilerParams(vmem_limit_bytes=10 * MIB),
        cost_estimate=SMALL,
        name="expert",
    )(*parts, *weights)


def add_kernel(parts, order, picking_ref, so_far_ref, gate_ref, *refs):
    inputs, out_ref, results = refs[:parts], refs[parts], refs[parts + 1]
    span = inputs[0].shape[0]
    places = []
    for number, (part, at) in enumerate(zip(inputs, order)):
        results[number * span : (number + 1) * span, :] = part[...]
        places.append(picking_ref[:, at * span : (at + 1) * span])
    picking = jnp.concatenate(places, axis=1) if parts > 1 else places[0]
    picked = jnp.dot(picking, results[...], preferred_element_type=jnp.float32)
    out_ref[...] = so_far_ref[...].astype(jnp.float32) + gate_ref[...] * picked


def close_kernel(parts, order, picking_ref, so_far_ref, gate_ref, gain_ref, *refs):
    *refs, out_hbm, results, total, out_ref, sems = refs
    add_kernel(parts, order, picking_ref, so_far_ref, gate_ref, *refs, total, results)
    copies = []
    for number, start in enumerate(range(0, total.shape[0], BLOCK)):
        rows = slice(start, start + BLOCK)
        out_ref[rows, :] = (normalise(total[rows, :]) * gain_ref[...]).astype(jnp.bfloat16)
        copies.append(
            pltpu.make_async_copy(
                out_ref.at[pl.ds(start, BLOCK), :], out_hbm.at[pl.ds(start, BLOCK), :], sems.at[number]
            )
        )
        copies[-1].start()
    for copy in copies:
        copy.wait()


def add_results(so_far, gate, picking, parts, gain=None):
    length, width = so_far.shape
    whole = pl.BlockSpec(memory_space=pltpu.VMEM)
    order, values = tuple(parts), [parts[at] for at in parts]
    span = values[0].shape[0]
    scratch = [pltpu.VMEM((span * len(parts), width), jnp.bfloat16)]
    last = gain is not None
    if last:
        scratch.append(pltpu.VMEM((length, width), jnp.float32))
        scratch.append(pltpu.VMEM((length, width), jnp.bfloat16))
        scratch.append(pltpu.SemaphoreType.DMA((length // BLOCK,)))
    return pl.pallas_call(
        functools.partial(close_kernel if last else add_kernel, len(parts), order),
        in_specs=[whole] * (3 + last + len(parts)),
        out_specs=pl.BlockSpec(memory_space=pl.ANY) if last else whole,
        out_shape=jax.ShapeDtypeStruct((length, width), jnp.bfloat16 if last else jnp.float32),
        scratch_shapes=scratch,
        compiler_params=pltpu.CompilerParams(vmem_limit_bytes=12 * MIB),
        cost_estimate=SMALL,
        name="finish" if last else "add",
    )(picking, so_far, gate, *([gain] if last else []), *values)


def on_device(frames, frame_counts, expert_ids, conv_kernel, router, w_in, w_out, final_gain):
    _, length, width = frames.shape
    n_dev = lax.axis_size("expert")
    chips = n_dev // 2
    cap = 2 * ((5 * length + 8 * chips - 1) // (8 * chips))
    chip = (lax.axis_index("expert") // 2).astype(jnp.int32).reshape(1)
    other_in = xor_route(w_in, "expert", 1)
    other_out = xor_route(w_out, "expert", 1)
    ids = expert_ids.reshape(1, length)
    gain = final_gain.reshape(1, width)

    if chips <= 8:
        pitch = -(-cap // 16) * 16
        own_in, own_out, stream, expert_in, slot, *messages = prepare(
            frames, frame_counts, chip, ids, conv_kernel, w_in, w_out, chips, cap, pitch, chips
        )
        send = lambda part, d: xor_route(part, "expert", 2 * d)
        far = [d for d in range(1, chips) if d >= chips // 2]
        near = [d for d in range(1, chips) if d < chips // 2]
        first, second = far[::2], far[1::2]
        arrived = {d: send(messages[d], d) for d in first}
        other_in, other_out = load(other_in, other_out)
        weights = (own_in, other_in, own_out, other_out)
        for d, part in zip(second, after([messages[d] for d in second], other_in)):
            arrived[d] = send(part, d)
        for d, part in zip(near, [messages[d] for d in near]):
            arrived[d] = send(part, d)
        first_out = run_expert([arrived[d] for d in first], weights)
        results = {}
        for d, part in zip(first, first_out):
            results[d] = send(part, d)
        gate, picking = gate_and_picking(frame_counts, expert_in, router, ids, slot, pitch)
        close = run_expert([messages[0]] + after([arrived[d] for d in near], first_out), weights)
        results[0] = close[0]
        second_out = run_expert(after([arrived[d] for d in second], (first_out, close)), weights)
        for d, part in zip(second, second_out):
            results[d] = send(part, d)
        for d, part in zip(near, close[1:]):
            results[d] = send(part, d)
        total = add_results(stream, gate, picking, {d: results[d] for d in [0] + first})
        total = add_results(total, gate, picking, {d: results[d] for d in near})
        output = add_results(total, gate, picking, {d: results[d] for d in second}, gain)
    else:
        home = jnp.zeros((1,), jnp.int32)
        own_in, own_out, stream, expert_in, slot, message = prepare(
            frames, frame_counts, home, ids, conv_kernel, w_in, w_out, chips, cap, cap, 1
        )
        gate, picking = gate_and_picking(frame_counts, expert_in, router, ids, slot, cap)
        other_in, other_out = load(other_in, other_out)
        (result,) = run_expert([exchange(message, "expert", chips)], (own_in, other_in, own_out, other_out))
        output = add_results(stream, gate, picking, {0: exchange(result, "expert", chips)}, gain)
    return output.reshape(1, length, width)


def solution(mesh):
    return jax.shard_map(
        on_device,
        mesh=mesh,
        in_specs=(
            P(("groups", "expert"), None, None),
            P(("groups", "expert")),
            P(("groups", "expert"), None, None),
            P(),
            P(),
            P(None, "expert"),
            P("expert", None),
            P(),
        ),
        out_specs=P(("groups", "expert"), None, None),
        check_vma=False,
    )
```

```python
import functools

import jax
import jax.numpy as jnp
from jax import lax
from jax.experimental import pallas as pl
from jax.experimental.pallas import tpu as pltpu
from jax.sharding import PartitionSpec as P

LANES = 128
ROWS = 8
BLOCK = 64
EPS = 1e-05
SMALL = pl.CostEstimate(flops=1, bytes_accessed=1, transcendentals=0)
MIB = 1 << 20


def xor_route(block, axis, distance):
    count = lax.axis_size(axis)
    return lax.ppermute(block, axis, [(i, i ^ distance) for i in range(count)])


def after(values, earlier):
    return lax.optimization_barrier((values, earlier))[0]


def exchange(block, axis, chips):
    count = lax.axis_size(axis)
    same_core = [list(range(core, count, 2)) for core in range(2)]
    blocks = block.reshape(chips, block.shape[0] // chips, block.shape[1])
    moved = lax.all_to_all(blocks, axis, split_axis=0, concat_axis=0, tiled=True, axis_index_groups=same_core)
    return moved.reshape(block.shape)


def in_hbm(array):
    return pltpu.with_memory_space_constraint(array, pltpu.HBM)


def silu(value):
    return 0.5 * value * (1.0 + jnp.tanh(0.5 * value))


def normalise(values):
    mean = jnp.mean(values, axis=-1, keepdims=True)
    centred = values - mean
    variance = jnp.mean(centred * centred, axis=-1, keepdims=True)
    return centred * lax.rsqrt(variance + EPS)


def pre_kernel(cap, pitch, count_ref, me_ref, frames_hbm, ids_hbm, taps_hbm, in_hbm, out_hbm, *rest):
    in_ref, out_ref, stream_ref, expert_in_ref, slot_ref, *rest = rest
    *message_refs, frames_ref, taps_ref, ids_ref, padded, taps_by_row, weights, pieces, conv = rest[:-4]
    frame_sems, taps_sem, ids_sem, weight_sems = rest[-4:]
    length, width = frames_ref.shape
    taps = taps_ref.shape[0]
    reach = taps // 2
    groups = width // LANES
    count = count_ref[0]

    frame_copies = [
        pltpu.make_async_copy(
            frames_hbm.at[0, pl.ds(start, BLOCK), :], frames_ref.at[pl.ds(start, BLOCK), :], frame_sems.at[number]
        )
        for number, start in enumerate(range(0, length, BLOCK))
    ]
    taps_copy = pltpu.make_async_copy(taps_hbm, taps_ref, taps_sem)
    for copy in frame_copies:
        copy.start()
    taps_copy.start()
    ids_copy = pltpu.make_async_copy(ids_hbm, ids_ref, ids_sem)
    ids_copy.start()
    weight_copies = [
        pltpu.make_async_copy(in_hbm, in_ref, weight_sems.at[0]),
        pltpu.make_async_copy(out_hbm, out_ref, weight_sems.at[1]),
    ]
    phases = 4
    depth = weights.shape[1] // groups
    edge = jnp.zeros((reach * groups, LANES), jnp.float32)
    padded[: reach * groups, :] = edge
    tail = (reach + length) * groups
    padded[tail:, :] = jnp.zeros((padded.shape[0] - tail, LANES), jnp.float32)
    taps_by_row[taps * groups :, :] = jnp.zeros(((phases * depth - taps) * groups, LANES), jnp.float32)
    taps_copy.wait()
    for group in range(groups):
        lanes = slice(group * LANES, (group + 1) * LANES)
        taps_by_row[pl.ds(group, taps, stride=groups), :] = taps_ref[:, lanes]
    for step in range(depth):
        w = [taps_by_row[(phases * step + i) * groups : (phases * step + i + 1) * groups, :] for i in range(phases)]
        halves = ((w[0] + w[1], w[2] + w[3]), (w[0], w[2]), (w[1], w[3]))
        for number, (even, odd) in enumerate(halves):
            for kind, value in enumerate((even + odd, even, odd)):
                weights[3 * number + kind, step * groups : (step + 1) * groups, :] = value

    for number, start in enumerate(range(0, length, BLOCK)):
        frame_copies[number].wait()
        values = frames_ref[start : start + BLOCK, :].astype(jnp.float32)
        position = start + lax.broadcasted_iota(jnp.int32, (BLOCK, 1), 0)
        normed = jnp.where(position < count, normalise(values), 0.0)
        for group in range(groups):
            lanes = slice(group * LANES, (group + 1) * LANES)
            padded[pl.ds((reach + start) * groups + group, BLOCK, stride=groups), :] = normed[:, lanes]
    for copy in weight_copies:
        copy.start()

    def split(index, carry):
        base = pl.multiple_of(index * (phases * ROWS * groups), phases * ROWS * groups)
        here = pl.multiple_of(index * (ROWS * groups), ROWS * groups)
        p = [padded[pl.ds(base + i * groups, groups), :] for i in range(phases * ROWS + 3)]
        pairs = 2 * ROWS + 1
        streams = (
            [p[2 * i + 1] for i in range(pairs)],
            [p[2 * i] - p[2 * i + 1] for i in range(pairs)],
            [p[2 * i + 2] - p[2 * i + 1] for i in range(pairs)],
        )
        for number, q in enumerate(streams):
            for row in range(ROWS):
                trio = (q[2 * row + 1], q[2 * row] - q[2 * row + 1], q[2 * row + 2] - q[2 * row + 1])
                for kind, value in enumerate(trio):
                    pieces[3 * number + kind, pl.ds(here + row * groups, groups), :] = value
        return carry

    lax.fori_loop(0, pieces.shape[1] // (ROWS * groups), split, 0)

    def correlate(index, carry):
        here = pl.multiple_of(index * (ROWS * groups), ROWS * groups)
        base = pl.multiple_of(index * (phases * ROWS * groups), phases * ROWS * groups)

        def piece(number):
            window = [pieces[number, pl.ds(here + i * groups, groups), :] for i in range(ROWS + depth - 1)]
            sums = None
            for step in range(depth):
                weight = weights[number, step * groups : (step + 1) * groups, :]
                terms = [weight * window[row + step] for row in range(ROWS)]
                sums = terms if sums is None else [a + b for a, b in zip(sums, terms)]
            return sums

        shared = piece(0)
        common = [[a + b for a, b in zip(shared, piece(1 + kind))] for kind in range(2)]
        for parity in range(2):
            shared = piece(3 + 3 * parity)
            for kind in range(2):
                last = piece(4 + 3 * parity + kind)
                for row in range(ROWS):
                    at = base + (phases * row + 2 * kind + parity) * groups
                    conv[pl.ds(at, groups), :] = (shared[row] + last[row]) + common[kind][row]
        return carry

    lax.fori_loop(0, length // (phases * ROWS), correlate, 0)

    for start in range(0, length, BLOCK):
        rows = slice(start, start + BLOCK)
        mixed = jnp.concatenate(
            [conv[pl.ds(start * groups + group, BLOCK, stride=groups), :] for group in range(groups)], axis=1
        )
        stream = (frames_ref[rows, :].astype(jnp.float32) + silu(mixed)).astype(jnp.bfloat16)
        stream_ref[rows, :] = stream
        expert_in_ref[rows, :] = normalise(stream.astype(jnp.float32)).astype(jnp.bfloat16)

    chips = slot_ref.shape[0]
    ids_copy.wait()
    ids = ids_ref[...] ^ me_ref[0]
    at = lax.broadcasted_iota(jnp.int32, (chips, length), 1)
    chosen = (ids == lax.broadcasted_iota(jnp.int32, (chips, length), 0)) & (at < count)
    earlier = lax.broadcasted_iota(jnp.int32, (length, length), 0) < lax.broadcasted_iota(
        jnp.int32, (length, length), 1
    )
    before = jnp.dot(
        chosen.astype(jnp.bfloat16), earlier.astype(jnp.bfloat16), preferred_element_type=jnp.float32
    )
    rank = jnp.sum(jnp.where(chosen, before, 0.0), axis=0, keepdims=True).astype(jnp.int32)
    sent = (at[:1] < count) & (rank < cap)
    slot = jnp.where(sent, ids * pitch + rank, -1)
    slot_ref[...] = jnp.broadcast_to(slot, slot_ref.shape)
    slots = chips * pitch
    placing = (slot == lax.broadcasted_iota(jnp.int32, (slots, length), 0)).astype(jnp.bfloat16)
    span = slots // len(message_refs)
    for start in range(0, width, 256):
        columns = slice(start, start + 256)
        placed = jnp.dot(placing, expert_in_ref[:, columns], preferred_element_type=jnp.float32)
        placed = placed.astype(jnp.bfloat16)
        for number, message in enumerate(message_refs):
            message[:, columns] = placed[number * span : (number + 1) * span, :]
    for copy in weight_copies:
        copy.wait()


def prepare(frames, count, me, ids, taps, w_in, w_out, chips, cap, pitch, messages):
    _, length, width = frames.shape
    groups = width // LANES
    reach = taps.shape[0] // 2
    whole = pl.BlockSpec(memory_space=pltpu.VMEM)
    anywhere = pl.BlockSpec(memory_space=pl.ANY)
    depth = -(-taps.shape[0] // 4)
    steps = length // 4 + -(-(depth - 1) // ROWS) * ROWS
    span = chips * pitch // messages
    bf16 = jnp.bfloat16
    return pl.pallas_call(
        functools.partial(pre_kernel, cap, pitch),
        in_specs=[pl.BlockSpec(memory_space=pltpu.SMEM)] * 2 + [anywhere] * 5,
        out_specs=[whole] * (5 + messages),
        out_shape=[
            pltpu.VMEM(w_in.shape, bf16),
            pltpu.VMEM(w_out.shape, bf16),
            jax.ShapeDtypeStruct((length, width), bf16),
            jax.ShapeDtypeStruct((length, width), bf16),
            jax.ShapeDtypeStruct((chips, length), jnp.int32),
        ]
        + [jax.ShapeDtypeStruct((span, width), bf16)] * messages,
        scratch_shapes=[
            pltpu.VMEM((length, width), bf16),
            pltpu.VMEM(taps.shape, jnp.float32),
            pltpu.VMEM(ids.shape, jnp.int32),
            pltpu.VMEM(((4 * steps + 8) * groups, LANES), jnp.float32),
            pltpu.VMEM((4 * depth * groups, LANES), jnp.float32),
            pltpu.VMEM((9, depth * groups, LANES), jnp.float32),
            pltpu.VMEM((9, steps * groups, LANES), jnp.float32),
            pltpu.VMEM((length * groups, LANES), jnp.float32),
            pltpu.SemaphoreType.DMA((length // BLOCK,)),
            pltpu.SemaphoreType.DMA,
            pltpu.SemaphoreType.DMA,
            pltpu.SemaphoreType.DMA((2,)),
        ],
        compiler_params=pltpu.CompilerParams(vmem_limit_bytes=12 * MIB),
        cost_estimate=SMALL,
        name="prepare",
    )(count, me, in_hbm(frames), in_hbm(ids), in_hbm(taps), in_hbm(w_in), in_hbm(w_out))


def load_kernel(count, *refs):
    sources, targets, sems = refs[:count], refs[count : 2 * count], refs[2 * count]
    copies = [pltpu.make_async_copy(a, b, sems.at[i]) for i, (a, b) in enumerate(zip(sources, targets))]
    for copy in copies:
        copy.start()
    for copy in copies:
        copy.wait()


def load(*arrays):
    count = len(arrays)
    return pl.pallas_call(
        functools.partial(load_kernel, count),
        in_specs=[pl.BlockSpec(memory_space=pl.ANY)] * count,
        out_specs=[pl.BlockSpec(memory_space=pltpu.VMEM)] * count,
        out_shape=[pltpu.VMEM(array.shape, array.dtype) for array in arrays],
        scratch_shapes=[pltpu.SemaphoreType.DMA((count,))],
        compiler_params=pltpu.CompilerParams(vmem_limit_bytes=4 * MIB),
        cost_estimate=SMALL,
        name="load",
    )(*[in_hbm(array) for array in arrays])


def gate_kernel(pitch, count_ref, expert_in_ref, router_ref, ids_ref, slot_ref, gate_ref, picking_ref):
    length = expert_in_ref.shape[0]
    experts = router_ref.shape[0]
    slots = picking_ref.shape[1]
    logits = lax.dot_general(
        expert_in_ref[...], router_ref[...], (((1,), (1,)), ((), ())), preferred_element_type=jnp.float32
    )
    ids = jnp.broadcast_to(ids_ref[...].astype(jnp.float32), (experts, length)).T
    position = lax.broadcasted_iota(jnp.int32, (length, experts), 0)
    column = lax.broadcasted_iota(jnp.int32, (length, experts), 1).astype(jnp.float32)
    chosen = (ids == column) & (position < count_ref[0])
    logit = jnp.sum(jnp.where(chosen, logits, 0.0), axis=1, keepdims=True)
    gate_ref[...] = 0.5 / (1.0 + jnp.exp(-logit))
    slot = slot_ref[...].astype(jnp.float32).T[:, :1].astype(jnp.int32)
    picking_ref[...] = (slot == lax.broadcasted_iota(jnp.int32, (length, slots), 1)).astype(jnp.bfloat16)


def gate_and_picking(count, expert_in, router, ids, slot, pitch):
    length = expert_in.shape[0]
    slots = slot.shape[0] * pitch
    whole = pl.BlockSpec(memory_space=pltpu.VMEM)
    return pl.pallas_call(
        functools.partial(gate_kernel, pitch),
        in_specs=[pl.BlockSpec(memory_space=pltpu.SMEM)] + [whole] * 4,
        out_specs=[whole] * 2,
        out_shape=[
            jax.ShapeDtypeStruct((length, 1), jnp.float32),
            jax.ShapeDtypeStruct((length, slots), jnp.bfloat16),
        ],
        compiler_params=pltpu.CompilerParams(vmem_limit_bytes=12 * MIB),
        cost_estimate=SMALL,
        name="gate",
    )(count, expert_in, router.T, ids, slot)


def expert_kernel(parts, tile, *refs):
    inputs, (in_a, in_b, out_a, out_b) = refs[:parts], refs[parts : parts + 4]
    outputs, (rows, total) = refs[parts + 4 : 2 * parts + 4], refs[2 * parts + 4 :]
    span = inputs[0].shape[0]
    for number, part in enumerate(inputs):
        rows[number * span : (number + 1) * span, :] = part[...]
    values = rows[...]
    hidden = in_a.shape[1]

    def step(index, carry):
        units = pl.ds(pl.multiple_of(index * tile, tile), tile)
        result = None
        for first, second in ((in_a, out_a), (in_b, out_b)):
            mid = silu(jnp.dot(values, first[:, units], preferred_element_type=jnp.float32)).astype(jnp.bfloat16)
            term = jnp.dot(mid, second[units, :], preferred_element_type=jnp.float32)
            result = term if result is None else result + term

        @pl.when(index == 0)
        def _():
            total[...] = result

        @pl.when(index > 0)
        def _():
            total[...] += result

        return carry

    lax.fori_loop(0, hidden // tile, step, 0)
    for number, part in enumerate(outputs):
        part[...] = total[number * span : (number + 1) * span, :].astype(jnp.bfloat16)


def run_expert(parts, weights):
    span, width = parts[0].shape
    whole = pl.BlockSpec(memory_space=pltpu.VMEM)
    count = len(parts)
    hidden = weights[0].shape[1]
    return pl.pallas_call(
        functools.partial(expert_kernel, count, min(1024, hidden)),
        in_specs=[whole] * (count + 4),
        out_specs=[whole] * count,
        out_shape=[jax.ShapeDtypeStruct((span, width), jnp.bfloat16)] * count,
        scratch_shapes=[
            pltpu.VMEM((span * count, width), jnp.bfloat16),
            pltpu.VMEM((span * count, width), jnp.float32),
        ],
        compiler_params=pltpu.CompilerParams(vmem_limit_bytes=10 * MIB),
        cost_estimate=SMALL,
        name="expert",
    )(*parts, *weights)


def add_kernel(parts, order, picking_ref, so_far_ref, gate_ref, *refs):
    inputs, out_ref, results = refs[:parts], refs[parts], refs[parts + 1]
    span = inputs[0].shape[0]
    places = []
    for number, (part, at) in enumerate(zip(inputs, order)):
        results[number * span : (number + 1) * span, :] = part[...]
        places.append(picking_ref[:, at * span : (at + 1) * span])
    picking = jnp.concatenate(places, axis=1) if parts > 1 else places[0]
    picked = jnp.dot(picking, results[...], preferred_element_type=jnp.float32)
    out_ref[...] = so_far_ref[...].astype(jnp.float32) + gate_ref[...] * picked


def close_kernel(parts, order, picking_ref, so_far_ref, gate_ref, gain_ref, *refs):
    *refs, out_hbm, results, total, out_ref, sems = refs
    add_kernel(parts, order, picking_ref, so_far_ref, gate_ref, *refs, total, results)
    copies = []
    for number, start in enumerate(range(0, total.shape[0], BLOCK)):
        rows = slice(start, start + BLOCK)
        out_ref[rows, :] = (normalise(total[rows, :]) * gain_ref[...]).astype(jnp.bfloat16)
        copies.append(
            pltpu.make_async_copy(
                out_ref.at[pl.ds(start, BLOCK), :], out_hbm.at[pl.ds(start, BLOCK), :], sems.at[number]
            )
        )
        copies[-1].start()
    for copy in copies:
        copy.wait()


def add_results(so_far, gate, picking, parts, gain=None):
    length, width = so_far.shape
    whole = pl.BlockSpec(memory_space=pltpu.VMEM)
    order, values = tuple(parts), [parts[at] for at in parts]
    span = values[0].shape[0]
    scratch = [pltpu.VMEM((span * len(parts), width), jnp.bfloat16)]
    last = gain is not None
    if last:
        scratch.append(pltpu.VMEM((length, width), jnp.float32))
        scratch.append(pltpu.VMEM((length, width), jnp.bfloat16))
        scratch.append(pltpu.SemaphoreType.DMA((length // BLOCK,)))
    return pl.pallas_call(
        functools.partial(close_kernel if last else add_kernel, len(parts), order),
        in_specs=[whole] * (3 + last + len(parts)),
        out_specs=pl.BlockSpec(memory_space=pl.ANY) if last else whole,
        out_shape=jax.ShapeDtypeStruct((length, width), jnp.bfloat16 if last else jnp.float32),
        scratch_shapes=scratch,
        compiler_params=pltpu.CompilerParams(vmem_limit_bytes=12 * MIB),
        cost_estimate=SMALL,
        name="finish" if last else "add",
    )(picking, so_far, gate, *([gain] if last else []), *values)


def on_device(frames, frame_counts, expert_ids, conv_kernel, router, w_in, w_out, final_gain):
    _, length, width = frames.shape
    n_dev = lax.axis_size("expert")
    chips = n_dev // 2
    cap = 2 * ((5 * length + 8 * chips - 1) // (8 * chips))
    chip = (lax.axis_index("expert") // 2).astype(jnp.int32).reshape(1)
    other_in = xor_route(w_in, "expert", 1)
    other_out = xor_route(w_out, "expert", 1)
    ids = expert_ids.reshape(1, length)
    gain = final_gain.reshape(1, width)

    if chips <= 8:
        pitch = -(-cap // 16) * 16
        own_in, own_out, stream, expert_in, slot, *messages = prepare(
            frames, frame_counts, chip, ids, conv_kernel, w_in, w_out, chips, cap, pitch, chips
        )
        send = lambda part, d: xor_route(part, "expert", 2 * d)
        far = [d for d in range(1, chips) if d >= chips // 2]
        near = [d for d in range(1, chips) if d < chips // 2]
        first, second = far[::2], far[1::2]
        arrived = {d: send(messages[d], d) for d in first}
        other_in, other_out = load(other_in, other_out)
        weights = (own_in, other_in, own_out, other_out)
        for d, part in zip(second, after([messages[d] for d in second], other_in)):
            arrived[d] = send(part, d)
        for d, part in zip(near, [messages[d] for d in near]):
            arrived[d] = send(part, d)
        first_out = run_expert([arrived[d] for d in first], weights)
        results = {}
        for d, part in zip(first, first_out):
            results[d] = send(part, d)
        gate, picking = gate_and_picking(frame_counts, expert_in, router, ids, slot, pitch)
        close = run_expert([messages[0]] + after([arrived[d] for d in near], first_out), weights)
        results[0] = close[0]
        second_out = run_expert(after([arrived[d] for d in second], (first_out, close)), weights)
        for d, part in zip(second, second_out):
            results[d] = send(part, d)
        for d, part in zip(near[:2], close[1:3]):
            results[d] = send(part, d)
        for d, part in zip(near[2:], after(close[3:], second_out)):
            results[d] = send(part, d)
        total = add_results(stream, gate, picking, {d: results[d] for d in [0] + first})
        total = add_results(total, gate, picking, {d: results[d] for d in near[:2]})
        output = add_results(total, gate, picking, {d: results[d] for d in second + near[2:]}, gain)
    else:
        home = jnp.zeros((1,), jnp.int32)
        own_in, own_out, stream, expert_in, slot, message = prepare(
            frames, frame_counts, home, ids, conv_kernel, w_in, w_out, chips, cap, cap, 1
        )
        gate, picking = gate_and_picking(frame_counts, expert_in, router, ids, slot, cap)
        other_in, other_out = load(other_in, other_out)
        (result,) = run_expert([exchange(message, "expert", chips)], (own_in, other_in, own_out, other_out))
        output = add_results(stream, gate, picking, {0: exchange(result, "expert", chips)}, gain)
    return output.reshape(1, length, width)


def solution(mesh):
    return jax.shard_map(
        on_device,
        mesh=mesh,
        in_specs=(
            P(("groups", "expert"), None, None),
            P(("groups", "expert")),
            P(("groups", "expert"), None, None),
            P(),
            P(),
            P(None, "expert"),
            P("expert", None),
            P(),
        ),
        out_specs=P(("groups", "expert"), None, None),
        check_vma=False,
    )
```

```python
import functools

import jax
import jax.numpy as jnp
from jax import lax
from jax.experimental import pallas as pl
from jax.experimental.pallas import tpu as pltpu
from jax.sharding import PartitionSpec as P

LANES = 128
ROWS = 8
BLOCK = 64
EPS = 1e-05
SMALL = pl.CostEstimate(flops=1, bytes_accessed=1, transcendentals=0)
MIB = 1 << 20


def xor_route(block, axis, distance):
    count = lax.axis_size(axis)
    return lax.ppermute(block, axis, [(i, i ^ distance) for i in range(count)])


def after(values, earlier):
    return lax.optimization_barrier((values, earlier))[0]


def exchange(block, axis, chips):
    count = lax.axis_size(axis)
    same_core = [list(range(core, count, 2)) for core in range(2)]
    blocks = block.reshape(chips, block.shape[0] // chips, block.shape[1])
    moved = lax.all_to_all(blocks, axis, split_axis=0, concat_axis=0, tiled=True, axis_index_groups=same_core)
    return moved.reshape(block.shape)


def in_hbm(array):
    return pltpu.with_memory_space_constraint(array, pltpu.HBM)


def silu(value):
    return 0.5 * value * (1.0 + jnp.tanh(0.5 * value))


def fold(values, rows):
    half = values.shape[1] // 2
    return jnp.concatenate([values[:rows, :half], values[:rows, half:]], axis=0)


def unfold(values):
    rows = values.shape[0] // 2
    values = values.astype(jnp.float32)
    return jnp.concatenate([values[:rows, :], values[rows:, :]], axis=1)


def pad_rows(values, rows):
    missing = rows - values.shape[0]
    if not missing:
        return values
    return jnp.concatenate([values, jnp.zeros((missing, values.shape[1]), values.dtype)], axis=0)


def read_part(part, width, pitch):
    values = part[...]
    if values.shape[1] == width:
        return values
    return pad_rows(unfold(values), pitch).astype(jnp.bfloat16)


def normalise(values):
    mean = jnp.mean(values, axis=-1, keepdims=True)
    centred = values - mean
    variance = jnp.mean(centred * centred, axis=-1, keepdims=True)
    return centred * lax.rsqrt(variance + EPS)


def pre_kernel(cap, pitch, count_ref, me_ref, frames_hbm, ids_hbm, taps_hbm, in_hbm, out_hbm, *rest):
    in_ref, out_ref, stream_ref, expert_in_ref, slot_ref, *rest = rest
    *message_refs, frames_ref, taps_ref, ids_ref, padded, taps_by_row, weights, pieces, conv = rest[:-4]
    frame_sems, taps_sem, ids_sem, weight_sems = rest[-4:]
    length, width = frames_ref.shape
    taps = taps_ref.shape[0]
    reach = taps // 2
    groups = width // LANES
    count = count_ref[0]

    frame_copies = [
        pltpu.make_async_copy(
            frames_hbm.at[0, pl.ds(start, BLOCK), :], frames_ref.at[pl.ds(start, BLOCK), :], frame_sems.at[number]
        )
        for number, start in enumerate(range(0, length, BLOCK))
    ]
    taps_copy = pltpu.make_async_copy(taps_hbm, taps_ref, taps_sem)
    for copy in frame_copies:
        copy.start()
    taps_copy.start()
    ids_copy = pltpu.make_async_copy(ids_hbm, ids_ref, ids_sem)
    ids_copy.start()
    weight_copies = [
        pltpu.make_async_copy(in_hbm, in_ref, weight_sems.at[0]),
        pltpu.make_async_copy(out_hbm, out_ref, weight_sems.at[1]),
    ]
    phases = 4
    depth = weights.shape[1] // groups
    edge = jnp.zeros((reach * groups, LANES), jnp.float32)
    padded[: reach * groups, :] = edge
    tail = (reach + length) * groups
    padded[tail:, :] = jnp.zeros((padded.shape[0] - tail, LANES), jnp.float32)
    taps_by_row[taps * groups :, :] = jnp.zeros(((phases * depth - taps) * groups, LANES), jnp.float32)
    taps_copy.wait()
    for group in range(groups):
        lanes = slice(group * LANES, (group + 1) * LANES)
        taps_by_row[pl.ds(group, taps, stride=groups), :] = taps_ref[:, lanes]
    for step in range(depth):
        w = [taps_by_row[(phases * step + i) * groups : (phases * step + i + 1) * groups, :] for i in range(phases)]
        halves = ((w[0] + w[1], w[2] + w[3]), (w[0], w[2]), (w[1], w[3]))
        for number, (even, odd) in enumerate(halves):
            for kind, value in enumerate((even + odd, even, odd)):
                weights[3 * number + kind, step * groups : (step + 1) * groups, :] = value

    for number, start in enumerate(range(0, length, BLOCK)):
        frame_copies[number].wait()
        values = frames_ref[start : start + BLOCK, :].astype(jnp.float32)
        position = start + lax.broadcasted_iota(jnp.int32, (BLOCK, 1), 0)
        normed = jnp.where(position < count, normalise(values), 0.0)
        for group in range(groups):
            lanes = slice(group * LANES, (group + 1) * LANES)
            padded[pl.ds((reach + start) * groups + group, BLOCK, stride=groups), :] = normed[:, lanes]
    for copy in weight_copies:
        copy.start()

    def split(index, carry):
        base = pl.multiple_of(index * (phases * ROWS * groups), phases * ROWS * groups)
        here = pl.multiple_of(index * (ROWS * groups), ROWS * groups)
        p = [padded[pl.ds(base + i * groups, groups), :] for i in range(phases * ROWS + 3)]
        pairs = 2 * ROWS + 1
        streams = (
            [p[2 * i + 1] for i in range(pairs)],
            [p[2 * i] - p[2 * i + 1] for i in range(pairs)],
            [p[2 * i + 2] - p[2 * i + 1] for i in range(pairs)],
        )
        for number, q in enumerate(streams):
            for row in range(ROWS):
                trio = (q[2 * row + 1], q[2 * row] - q[2 * row + 1], q[2 * row + 2] - q[2 * row + 1])
                for kind, value in enumerate(trio):
                    pieces[3 * number + kind, pl.ds(here + row * groups, groups), :] = value
        return carry

    lax.fori_loop(0, pieces.shape[1] // (ROWS * groups), split, 0)

    def correlate(index, carry):
        here = pl.multiple_of(index * (ROWS * groups), ROWS * groups)
        base = pl.multiple_of(index * (phases * ROWS * groups), phases * ROWS * groups)

        def piece(number):
            window = [pieces[number, pl.ds(here + i * groups, groups), :] for i in range(ROWS + depth - 1)]
            sums = None
            for step in range(depth):
                weight = weights[number, step * groups : (step + 1) * groups, :]
                terms = [weight * window[row + step] for row in range(ROWS)]
                sums = terms if sums is None else [a + b for a, b in zip(sums, terms)]
            return sums

        shared = piece(0)
        common = [[a + b for a, b in zip(shared, piece(1 + kind))] for kind in range(2)]
        for parity in range(2):
            shared = piece(3 + 3 * parity)
            for kind in range(2):
                last = piece(4 + 3 * parity + kind)
                for row in range(ROWS):
                    at = base + (phases * row + 2 * kind + parity) * groups
                    conv[pl.ds(at, groups), :] = (shared[row] + last[row]) + common[kind][row]
        return carry

    lax.fori_loop(0, length // (phases * ROWS), correlate, 0)

    for start in range(0, length, BLOCK):
        rows = slice(start, start + BLOCK)
        mixed = jnp.concatenate(
            [conv[pl.ds(start * groups + group, BLOCK, stride=groups), :] for group in range(groups)], axis=1
        )
        stream = (frames_ref[rows, :].astype(jnp.float32) + silu(mixed)).astype(jnp.bfloat16)
        stream_ref[rows, :] = stream
        expert_in_ref[rows, :] = normalise(stream.astype(jnp.float32)).astype(jnp.bfloat16)

    chips = slot_ref.shape[0]
    ids_copy.wait()
    ids = ids_ref[...] ^ me_ref[0]
    at = lax.broadcasted_iota(jnp.int32, (chips, length), 1)
    chosen = (ids == lax.broadcasted_iota(jnp.int32, (chips, length), 0)) & (at < count)
    earlier = lax.broadcasted_iota(jnp.int32, (length, length), 0) < lax.broadcasted_iota(
        jnp.int32, (length, length), 1
    )
    before = jnp.dot(
        chosen.astype(jnp.bfloat16), earlier.astype(jnp.bfloat16), preferred_element_type=jnp.float32
    )
    rank = jnp.sum(jnp.where(chosen, before, 0.0), axis=0, keepdims=True).astype(jnp.int32)
    sent = (at[:1] < count) & (rank < cap)
    slot = jnp.where(sent, ids * pitch + rank, -1)
    slot_ref[...] = jnp.broadcast_to(slot, slot_ref.shape)
    slots = chips * pitch
    placing = (slot == lax.broadcasted_iota(jnp.int32, (slots, length), 0)).astype(jnp.bfloat16)
    span = slots // len(message_refs)
    folded = message_refs[0].shape[1] != width
    part = width // 4
    for start in range(0, width // 2 if folded else width, part):
        placed = [
            jnp.dot(placing, expert_in_ref[:, at : at + part], preferred_element_type=jnp.float32)
            for at in ((start, width // 2 + start) if folded else (start,))
        ]
        for number, message in enumerate(message_refs):
            rows = slice(number * span, (number + 1) * span)
            value = placed[0][rows, :]
            if folded:
                value = fold(jnp.concatenate([value, placed[1][rows, :]], axis=1), cap)
            message[:, start : start + part] = value.astype(jnp.bfloat16)
    for copy in weight_copies:
        copy.wait()


def prepare(frames, count, me, ids, taps, w_in, w_out, chips, cap, pitch, messages, folded):
    _, length, width = frames.shape
    groups = width // LANES
    reach = taps.shape[0] // 2
    whole = pl.BlockSpec(memory_space=pltpu.VMEM)
    anywhere = pl.BlockSpec(memory_space=pl.ANY)
    depth = -(-taps.shape[0] // 4)
    steps = length // 4 + -(-(depth - 1) // ROWS) * ROWS
    span = chips * pitch // messages
    bf16 = jnp.bfloat16
    return pl.pallas_call(
        functools.partial(pre_kernel, cap, pitch),
        in_specs=[pl.BlockSpec(memory_space=pltpu.SMEM)] * 2 + [anywhere] * 5,
        out_specs=[whole] * (5 + messages),
        out_shape=[
            pltpu.VMEM(w_in.shape, bf16),
            pltpu.VMEM(w_out.shape, bf16),
            jax.ShapeDtypeStruct((length, width), bf16),
            jax.ShapeDtypeStruct((length, width), bf16),
            jax.ShapeDtypeStruct((chips, length), jnp.int32),
        ]
        + [jax.ShapeDtypeStruct((2 * cap, width // 2) if folded else (span, width), bf16)] * messages,
        scratch_shapes=[
            pltpu.VMEM((length, width), bf16),
            pltpu.VMEM(taps.shape, jnp.float32),
            pltpu.VMEM(ids.shape, jnp.int32),
            pltpu.VMEM(((4 * steps + 8) * groups, LANES), jnp.float32),
            pltpu.VMEM((4 * depth * groups, LANES), jnp.float32),
            pltpu.VMEM((9, depth * groups, LANES), jnp.float32),
            pltpu.VMEM((9, steps * groups, LANES), jnp.float32),
            pltpu.VMEM((length * groups, LANES), jnp.float32),
            pltpu.SemaphoreType.DMA((length // BLOCK,)),
            pltpu.SemaphoreType.DMA,
            pltpu.SemaphoreType.DMA,
            pltpu.SemaphoreType.DMA((2,)),
        ],
        compiler_params=pltpu.CompilerParams(vmem_limit_bytes=12 * MIB),
        cost_estimate=SMALL,
        name="prepare",
    )(count, me, in_hbm(frames), in_hbm(ids), in_hbm(taps), in_hbm(w_in), in_hbm(w_out))


def load_kernel(count, *refs):
    sources, targets, sems = refs[:count], refs[count : 2 * count], refs[2 * count]
    copies = [pltpu.make_async_copy(a, b, sems.at[i]) for i, (a, b) in enumerate(zip(sources, targets))]
    for copy in copies:
        copy.start()
    for copy in copies:
        copy.wait()


def load(*arrays):
    count = len(arrays)
    return pl.pallas_call(
        functools.partial(load_kernel, count),
        in_specs=[pl.BlockSpec(memory_space=pl.ANY)] * count,
        out_specs=[pl.BlockSpec(memory_space=pltpu.VMEM)] * count,
        out_shape=[pltpu.VMEM(array.shape, array.dtype) for array in arrays],
        scratch_shapes=[pltpu.SemaphoreType.DMA((count,))],
        compiler_params=pltpu.CompilerParams(vmem_limit_bytes=4 * MIB),
        cost_estimate=SMALL,
        name="load",
    )(*[in_hbm(array) for array in arrays])


def gate_kernel(pitch, count_ref, expert_in_ref, router_ref, ids_ref, slot_ref, gate_ref, picking_ref):
    length = expert_in_ref.shape[0]
    experts = router_ref.shape[0]
    slots = picking_ref.shape[1]
    logits = lax.dot_general(
        expert_in_ref[...], router_ref[...], (((1,), (1,)), ((), ())), preferred_element_type=jnp.float32
    )
    ids = jnp.broadcast_to(ids_ref[...].astype(jnp.float32), (experts, length)).T
    position = lax.broadcasted_iota(jnp.int32, (length, experts), 0)
    column = lax.broadcasted_iota(jnp.int32, (length, experts), 1).astype(jnp.float32)
    chosen = (ids == column) & (position < count_ref[0])
    logit = jnp.sum(jnp.where(chosen, logits, 0.0), axis=1, keepdims=True)
    gate_ref[...] = 0.5 / (1.0 + jnp.exp(-logit))
    slot = slot_ref[...].astype(jnp.float32).T[:, :1].astype(jnp.int32)
    picking_ref[...] = (slot == lax.broadcasted_iota(jnp.int32, (length, slots), 1)).astype(jnp.bfloat16)


def gate_and_picking(count, expert_in, router, ids, slot, pitch):
    length = expert_in.shape[0]
    slots = slot.shape[0] * pitch
    whole = pl.BlockSpec(memory_space=pltpu.VMEM)
    return pl.pallas_call(
        functools.partial(gate_kernel, pitch),
        in_specs=[pl.BlockSpec(memory_space=pltpu.SMEM)] + [whole] * 4,
        out_specs=[whole] * 2,
        out_shape=[
            jax.ShapeDtypeStruct((length, 1), jnp.float32),
            jax.ShapeDtypeStruct((length, slots), jnp.bfloat16),
        ],
        compiler_params=pltpu.CompilerParams(vmem_limit_bytes=12 * MIB),
        cost_estimate=SMALL,
        name="gate",
    )(count, expert_in, router.T, ids, slot)


def expert_kernel(parts, span, tile, *refs):
    inputs, (in_a, in_b, out_a, out_b) = refs[:parts], refs[parts : parts + 4]
    outputs, (rows, total) = refs[parts + 4 : 2 * parts + 4], refs[2 * parts + 4 :]
    width = rows.shape[1]
    for number, part in enumerate(inputs):
        rows[number * span : (number + 1) * span, :] = read_part(part, width, span)
    values = rows[...]
    hidden = in_a.shape[1]

    def step(index, carry):
        units = pl.ds(pl.multiple_of(index * tile, tile), tile)
        result = None
        for first, second in ((in_a, out_a), (in_b, out_b)):
            mid = silu(jnp.dot(values, first[:, units], preferred_element_type=jnp.float32)).astype(jnp.bfloat16)
            term = jnp.dot(mid, second[units, :], preferred_element_type=jnp.float32)
            result = term if result is None else result + term

        @pl.when(index == 0)
        def _():
            total[...] = result

        @pl.when(index > 0)
        def _():
            total[...] += result

        return carry

    lax.fori_loop(0, hidden // tile, step, 0)
    for number, part in enumerate(outputs):
        value = total[number * span : (number + 1) * span, :]
        if part.shape[1] != width:
            value = fold(value, part.shape[0] // 2)
        part[...] = value.astype(jnp.bfloat16)


def run_expert(parts, weights, span):
    width = weights[0].shape[0]
    whole = pl.BlockSpec(memory_space=pltpu.VMEM)
    count = len(parts)
    hidden = weights[0].shape[1]
    return pl.pallas_call(
        functools.partial(expert_kernel, count, span, min(1024, hidden)),
        in_specs=[whole] * (count + 4),
        out_specs=[whole] * count,
        out_shape=[jax.ShapeDtypeStruct(parts[0].shape, jnp.bfloat16)] * count,
        scratch_shapes=[
            pltpu.VMEM((span * count, width), jnp.bfloat16),
            pltpu.VMEM((span * count, width), jnp.float32),
        ],
        compiler_params=pltpu.CompilerParams(vmem_limit_bytes=10 * MIB),
        cost_estimate=SMALL,
        name="expert",
    )(*parts, *weights)


def add_kernel(parts, order, span, picking_ref, so_far_ref, gate_ref, *refs):
    inputs, out_ref, results = refs[:parts], refs[parts], refs[parts + 1]
    places = []
    for number, (part, at) in enumerate(zip(inputs, order)):
        results[number * span : (number + 1) * span, :] = read_part(part, results.shape[1], span)
        places.append(picking_ref[:, at * span : (at + 1) * span])
    picking = jnp.concatenate(places, axis=1) if parts > 1 else places[0]
    picked = jnp.dot(picking, results[...], preferred_element_type=jnp.float32)
    out_ref[...] = so_far_ref[...].astype(jnp.float32) + gate_ref[...] * picked


def close_kernel(parts, order, span, picking_ref, so_far_ref, gate_ref, gain_ref, *refs):
    *refs, out_hbm, results, total, out_ref, sems = refs
    add_kernel(parts, order, span, picking_ref, so_far_ref, gate_ref, *refs, total, results)
    copies = []
    for number, start in enumerate(range(0, total.shape[0], BLOCK)):
        rows = slice(start, start + BLOCK)
        out_ref[rows, :] = (normalise(total[rows, :]) * gain_ref[...]).astype(jnp.bfloat16)
        copies.append(
            pltpu.make_async_copy(
                out_ref.at[pl.ds(start, BLOCK), :], out_hbm.at[pl.ds(start, BLOCK), :], sems.at[number]
            )
        )
        copies[-1].start()
    for copy in copies:
        copy.wait()


def add_results(so_far, gate, picking, parts, span, gain=None):
    length, width = so_far.shape
    whole = pl.BlockSpec(memory_space=pltpu.VMEM)
    order, values = tuple(parts), [parts[at] for at in parts]
    scratch = [pltpu.VMEM((span * len(parts), width), jnp.bfloat16)]
    last = gain is not None
    if last:
        scratch.append(pltpu.VMEM((length, width), jnp.float32))
        scratch.append(pltpu.VMEM((length, width), jnp.bfloat16))
        scratch.append(pltpu.SemaphoreType.DMA((length // BLOCK,)))
    return pl.pallas_call(
        functools.partial(close_kernel if last else add_kernel, len(parts), order, span),
        in_specs=[whole] * (3 + last + len(parts)),
        out_specs=pl.BlockSpec(memory_space=pl.ANY) if last else whole,
        out_shape=jax.ShapeDtypeStruct((length, width), jnp.bfloat16 if last else jnp.float32),
        scratch_shapes=scratch,
        compiler_params=pltpu.CompilerParams(vmem_limit_bytes=12 * MIB),
        cost_estimate=SMALL,
        name="finish" if last else "add",
    )(picking, so_far, gate, *([gain] if last else []), *values)


def on_device(frames, frame_counts, expert_ids, conv_kernel, router, w_in, w_out, final_gain):
    _, length, width = frames.shape
    n_dev = lax.axis_size("expert")
    chips = n_dev // 2
    cap = 2 * ((5 * length + 8 * chips - 1) // (8 * chips))
    chip = (lax.axis_index("expert") // 2).astype(jnp.int32).reshape(1)
    other_in = xor_route(w_in, "expert", 1)
    other_out = xor_route(w_out, "expert", 1)
    ids = expert_ids.reshape(1, length)
    gain = final_gain.reshape(1, width)

    if chips <= 8:
        pitch = -(-cap // 16) * 16
        folded = cap % 8 == 4
        own_in, own_out, stream, expert_in, slot, *messages = prepare(
            frames, frame_counts, chip, ids, conv_kernel, w_in, w_out, chips, cap, pitch, chips, folded
        )
        send = lambda part, d: xor_route(part, "expert", 2 * d)
        far = [d for d in range(1, chips) if d >= chips // 2]
        near = [d for d in range(1, chips) if d < chips // 2]
        first, second = far[::2], far[1::2]
        arrived = {d: send(messages[d], d) for d in first}
        other_in, other_out = load(other_in, other_out)
        weights = (own_in, other_in, own_out, other_out)
        for d, part in zip(second, after([messages[d] for d in second], other_in)):
            arrived[d] = send(part, d)
        for d, part in zip(near, [messages[d] for d in near]):
            arrived[d] = send(part, d)
        first_out = run_expert([arrived[d] for d in first], weights, pitch)
        results = {}
        for d, part in zip(first, first_out):
            results[d] = send(part, d)
        gate, picking = gate_and_picking(frame_counts, expert_in, router, ids, slot, pitch)
        close = run_expert([messages[0]] + after([arrived[d] for d in near], first_out), weights, pitch)
        results[0] = close[0]
        second_out = run_expert(after([arrived[d] for d in second], (first_out, close)), weights, pitch)
        for d, part in zip(second, second_out):
            results[d] = send(part, d)
        for d, part in zip(near[:2], close[1:3]):
            results[d] = send(part, d)
        for d, part in zip(near[2:], after(close[3:], second_out)):
            results[d] = send(part, d)
        total = add_results(stream, gate, picking, {d: results[d] for d in [0] + first}, pitch)
        total = add_results(total, gate, picking, {d: results[d] for d in near[:2]}, pitch)
        output = add_results(total, gate, picking, {d: results[d] for d in second + near[2:]}, pitch, gain)
    else:
        home = jnp.zeros((1,), jnp.int32)
        own_in, own_out, stream, expert_in, slot, message = prepare(
            frames, frame_counts, home, ids, conv_kernel, w_in, w_out, chips, cap, cap, 1, False
        )
        gate, picking = gate_and_picking(frame_counts, expert_in, router, ids, slot, cap)
        other_in, other_out = load(other_in, other_out)
        (result,) = run_expert([exchange(message, "expert", chips)], (own_in, other_in, own_out, other_out), chips * cap)
        output = add_results(stream, gate, picking, {0: exchange(result, "expert", chips)}, chips * cap, gain)
    return output.reshape(1, length, width)


def solution(mesh):
    return jax.shard_map(
        on_device,
        mesh=mesh,
        in_specs=(
            P(("groups", "expert"), None, None),
            P(("groups", "expert")),
            P(("groups", "expert"), None, None),
            P(),
            P(),
            P(None, "expert"),
            P("expert", None),
            P(),
        ),
        out_specs=P(("groups", "expert"), None, None),
        check_vma=False,
    )
```

```python
import functools

import jax
import jax.numpy as jnp
from jax import lax
from jax.experimental import pallas as pl
from jax.experimental.pallas import tpu as pltpu
from jax.sharding import PartitionSpec as P

LANES = 128
ROWS = 8
BLOCK = 64
EPS = 1e-05
SMALL = pl.CostEstimate(flops=1, bytes_accessed=1, transcendentals=0)
MIB = 1 << 20


def xor_route(block, axis, distance):
    count = lax.axis_size(axis)
    return lax.ppermute(block, axis, [(i, i ^ distance) for i in range(count)])


def after(values, earlier):
    return lax.optimization_barrier((values, earlier))[0]


def exchange(block, axis, chips):
    count = lax.axis_size(axis)
    same_core = [list(range(core, count, 2)) for core in range(2)]
    blocks = block.reshape(chips, block.shape[0] // chips, block.shape[1])
    moved = lax.all_to_all(blocks, axis, split_axis=0, concat_axis=0, tiled=True, axis_index_groups=same_core)
    return moved.reshape(block.shape)


def in_hbm(array):
    return pltpu.with_memory_space_constraint(array, pltpu.HBM)


def silu(value):
    return 0.5 * value * (1.0 + jnp.tanh(0.5 * value))


def fold(values, rows):
    half = values.shape[1] // 2
    return jnp.concatenate([values[:rows, :half], values[:rows, half:]], axis=0)


def unfold(values):
    rows = values.shape[0] // 2
    values = values.astype(jnp.float32)
    return jnp.concatenate([values[:rows, :], values[rows:, :]], axis=1)


def pad_rows(values, rows):
    missing = rows - values.shape[0]
    if not missing:
        return values
    return jnp.concatenate([values, jnp.zeros((missing, values.shape[1]), values.dtype)], axis=0)


def read_part(part, width, pitch):
    values = part[...]
    if values.shape[1] == width:
        return values
    return pad_rows(unfold(values), pitch).astype(jnp.bfloat16)


def normalise(values):
    mean = jnp.mean(values, axis=-1, keepdims=True)
    centred = values - mean
    variance = jnp.mean(centred * centred, axis=-1, keepdims=True)
    return centred * lax.rsqrt(variance + EPS)


def pre_kernel(cap, pitch, count_ref, me_ref, frames_hbm, ids_hbm, taps_hbm, in_hbm, out_hbm, *rest):
    in_ref, out_ref, stream_ref, expert_in_ref, slot_ref, *rest = rest
    *message_refs, frames_ref, taps_ref, ids_ref, padded, taps_by_row, weights, pieces, conv = rest[:-4]
    frame_sems, taps_sem, ids_sem, weight_sems = rest[-4:]
    length, width = frames_ref.shape
    taps = taps_ref.shape[0]
    reach = taps // 2
    groups = width // LANES
    count = count_ref[0]

    frame_copies = [
        pltpu.make_async_copy(
            frames_hbm.at[0, pl.ds(start, BLOCK), :], frames_ref.at[pl.ds(start, BLOCK), :], frame_sems.at[number]
        )
        for number, start in enumerate(range(0, length, BLOCK))
    ]
    taps_copy = pltpu.make_async_copy(taps_hbm, taps_ref, taps_sem)
    for copy in frame_copies:
        copy.start()
    taps_copy.start()
    ids_copy = pltpu.make_async_copy(ids_hbm, ids_ref, ids_sem)
    ids_copy.start()
    weight_copies = [
        pltpu.make_async_copy(in_hbm, in_ref, weight_sems.at[0]),
        pltpu.make_async_copy(out_hbm, out_ref, weight_sems.at[1]),
    ]
    phases = 4
    depth = weights.shape[1] // groups
    edge = jnp.zeros((reach * groups, LANES), jnp.float32)
    padded[: reach * groups, :] = edge
    tail = (reach + length) * groups
    padded[tail:, :] = jnp.zeros((padded.shape[0] - tail, LANES), jnp.float32)
    taps_by_row[taps * groups :, :] = jnp.zeros(((phases * depth - taps) * groups, LANES), jnp.float32)
    taps_copy.wait()
    for group in range(groups):
        lanes = slice(group * LANES, (group + 1) * LANES)
        taps_by_row[pl.ds(group, taps, stride=groups), :] = taps_ref[:, lanes]
    for step in range(depth):
        w = [taps_by_row[(phases * step + i) * groups : (phases * step + i + 1) * groups, :] for i in range(phases)]
        halves = ((w[0] + w[1], w[2] + w[3]), (w[0], w[2]), (w[1], w[3]))
        for number, (even, odd) in enumerate(halves):
            for kind, value in enumerate((even + odd, even, odd)):
                weights[3 * number + kind, step * groups : (step + 1) * groups, :] = value

    for number, start in enumerate(range(0, length, BLOCK)):
        frame_copies[number].wait()
        values = frames_ref[start : start + BLOCK, :].astype(jnp.float32)
        position = start + lax.broadcasted_iota(jnp.int32, (BLOCK, 1), 0)
        normed = jnp.where(position < count, normalise(values), 0.0)
        for group in range(groups):
            lanes = slice(group * LANES, (group + 1) * LANES)
            padded[pl.ds((reach + start) * groups + group, BLOCK, stride=groups), :] = normed[:, lanes]
    for copy in weight_copies:
        copy.start()

    def split(index, carry):
        base = pl.multiple_of(index * (phases * ROWS * groups), phases * ROWS * groups)
        here = pl.multiple_of(index * (ROWS * groups), ROWS * groups)
        p = [padded[pl.ds(base + i * groups, groups), :] for i in range(phases * ROWS + 3)]
        pairs = 2 * ROWS + 1
        streams = (
            [p[2 * i + 1] for i in range(pairs)],
            [p[2 * i] - p[2 * i + 1] for i in range(pairs)],
            [p[2 * i + 2] - p[2 * i + 1] for i in range(pairs)],
        )
        for number, q in enumerate(streams):
            for row in range(ROWS):
                trio = (q[2 * row + 1], q[2 * row] - q[2 * row + 1], q[2 * row + 2] - q[2 * row + 1])
                for kind, value in enumerate(trio):
                    pieces[3 * number + kind, pl.ds(here + row * groups, groups), :] = value
        return carry

    lax.fori_loop(0, pieces.shape[1] // (ROWS * groups), split, 0)

    def correlate(index, carry):
        here = pl.multiple_of(index * (ROWS * groups), ROWS * groups)
        base = pl.multiple_of(index * (phases * ROWS * groups), phases * ROWS * groups)

        def piece(number):
            window = [pieces[number, pl.ds(here + i * groups, groups), :] for i in range(ROWS + depth - 1)]
            sums = None
            for step in range(depth):
                weight = weights[number, step * groups : (step + 1) * groups, :]
                terms = [weight * window[row + step] for row in range(ROWS)]
                sums = terms if sums is None else [a + b for a, b in zip(sums, terms)]
            return sums

        shared = piece(0)
        common = [[a + b for a, b in zip(shared, piece(1 + kind))] for kind in range(2)]
        for parity in range(2):
            shared = piece(3 + 3 * parity)
            for kind in range(2):
                last = piece(4 + 3 * parity + kind)
                for row in range(ROWS):
                    at = base + (phases * row + 2 * kind + parity) * groups
                    conv[pl.ds(at, groups), :] = (shared[row] + last[row]) + common[kind][row]
        return carry

    lax.fori_loop(0, length // (phases * ROWS), correlate, 0)

    for start in range(0, length, BLOCK):
        rows = slice(start, start + BLOCK)
        mixed = jnp.concatenate(
            [conv[pl.ds(start * groups + group, BLOCK, stride=groups), :] for group in range(groups)], axis=1
        )
        stream = (frames_ref[rows, :].astype(jnp.float32) + silu(mixed)).astype(jnp.bfloat16)
        stream_ref[rows, :] = stream
        expert_in_ref[rows, :] = normalise(stream.astype(jnp.float32)).astype(jnp.bfloat16)

    chips = slot_ref.shape[0]
    ids_copy.wait()
    ids = ids_ref[...] ^ me_ref[0]
    at = lax.broadcasted_iota(jnp.int32, (chips, length), 1)
    chosen = (ids == lax.broadcasted_iota(jnp.int32, (chips, length), 0)) & (at < count)
    earlier = lax.broadcasted_iota(jnp.int32, (length, length), 0) < lax.broadcasted_iota(
        jnp.int32, (length, length), 1
    )
    before = jnp.dot(
        chosen.astype(jnp.bfloat16), earlier.astype(jnp.bfloat16), preferred_element_type=jnp.float32
    )
    rank = jnp.sum(jnp.where(chosen, before, 0.0), axis=0, keepdims=True).astype(jnp.int32)
    sent = (at[:1] < count) & (rank < cap)
    slot = jnp.where(sent, ids * pitch + rank, -1)
    slot_ref[...] = jnp.broadcast_to(slot, slot_ref.shape)
    slots = chips * pitch
    placing = (slot == lax.broadcasted_iota(jnp.int32, (slots, length), 0)).astype(jnp.bfloat16)
    span = slots // len(message_refs)
    folded = message_refs[0].shape[1] != width
    part = width // 4
    for start in range(0, width // 2 if folded else width, part):
        placed = [
            jnp.dot(placing, expert_in_ref[:, at : at + part], preferred_element_type=jnp.float32)
            for at in ((start, width // 2 + start) if folded else (start,))
        ]
        for number, message in enumerate(message_refs):
            rows = slice(number * span, (number + 1) * span)
            value = placed[0][rows, :]
            if folded:
                value = fold(jnp.concatenate([value, placed[1][rows, :]], axis=1), cap)
            message[:, start : start + part] = value.astype(jnp.bfloat16)
    for copy in weight_copies:
        copy.wait()


def prepare(frames, count, me, ids, taps, w_in, w_out, chips, cap, pitch, messages, folded):
    _, length, width = frames.shape
    groups = width // LANES
    reach = taps.shape[0] // 2
    whole = pl.BlockSpec(memory_space=pltpu.VMEM)
    anywhere = pl.BlockSpec(memory_space=pl.ANY)
    depth = -(-taps.shape[0] // 4)
    steps = length // 4 + -(-(depth - 1) // ROWS) * ROWS
    span = chips * pitch // messages
    bf16 = jnp.bfloat16
    return pl.pallas_call(
        functools.partial(pre_kernel, cap, pitch),
        in_specs=[pl.BlockSpec(memory_space=pltpu.SMEM)] * 2 + [anywhere] * 5,
        out_specs=[whole] * (5 + messages),
        out_shape=[
            pltpu.VMEM(w_in.shape, bf16),
            pltpu.VMEM(w_out.shape, bf16),
            jax.ShapeDtypeStruct((length, width), bf16),
            jax.ShapeDtypeStruct((length, width), bf16),
            jax.ShapeDtypeStruct((chips, length), jnp.int32),
        ]
        + [jax.ShapeDtypeStruct((2 * cap, width // 2) if folded else (span, width), bf16)] * messages,
        scratch_shapes=[
            pltpu.VMEM((length, width), bf16),
            pltpu.VMEM(taps.shape, jnp.float32),
            pltpu.VMEM(ids.shape, jnp.int32),
            pltpu.VMEM(((4 * steps + 8) * groups, LANES), jnp.float32),
            pltpu.VMEM((4 * depth * groups, LANES), jnp.float32),
            pltpu.VMEM((9, depth * groups, LANES), jnp.float32),
            pltpu.VMEM((9, steps * groups, LANES), jnp.float32),
            pltpu.VMEM((length * groups, LANES), jnp.float32),
            pltpu.SemaphoreType.DMA((length // BLOCK,)),
            pltpu.SemaphoreType.DMA,
            pltpu.SemaphoreType.DMA,
            pltpu.SemaphoreType.DMA((2,)),
        ],
        compiler_params=pltpu.CompilerParams(vmem_limit_bytes=12 * MIB),
        cost_estimate=SMALL,
        name="prepare",
    )(count, me, in_hbm(frames), in_hbm(ids), in_hbm(taps), in_hbm(w_in), in_hbm(w_out))


def load_kernel(count, *refs):
    sources, targets, sems = refs[:count], refs[count : 2 * count], refs[2 * count]
    copies = [pltpu.make_async_copy(a, b, sems.at[i]) for i, (a, b) in enumerate(zip(sources, targets))]
    for copy in copies:
        copy.start()
    for copy in copies:
        copy.wait()


def load(*arrays):
    count = len(arrays)
    return pl.pallas_call(
        functools.partial(load_kernel, count),
        in_specs=[pl.BlockSpec(memory_space=pl.ANY)] * count,
        out_specs=[pl.BlockSpec(memory_space=pltpu.VMEM)] * count,
        out_shape=[pltpu.VMEM(array.shape, array.dtype) for array in arrays],
        scratch_shapes=[pltpu.SemaphoreType.DMA((count,))],
        compiler_params=pltpu.CompilerParams(vmem_limit_bytes=4 * MIB),
        cost_estimate=SMALL,
        name="load",
    )(*[in_hbm(array) for array in arrays])


def gate_kernel(pitch, count_ref, expert_in_ref, router_ref, ids_ref, slot_ref, gate_ref, picking_ref):
    length = expert_in_ref.shape[0]
    experts = router_ref.shape[0]
    slots = picking_ref.shape[1]
    logits = lax.dot_general(
        expert_in_ref[...], router_ref[...], (((1,), (1,)), ((), ())), preferred_element_type=jnp.float32
    )
    ids = jnp.broadcast_to(ids_ref[...].astype(jnp.float32), (experts, length)).T
    position = lax.broadcasted_iota(jnp.int32, (length, experts), 0)
    column = lax.broadcasted_iota(jnp.int32, (length, experts), 1).astype(jnp.float32)
    chosen = (ids == column) & (position < count_ref[0])
    logit = jnp.sum(jnp.where(chosen, logits, 0.0), axis=1, keepdims=True)
    gate_ref[...] = 0.5 / (1.0 + jnp.exp(-logit))
    slot = slot_ref[...].astype(jnp.float32).T[:, :1].astype(jnp.int32)
    picking_ref[...] = (slot == lax.broadcasted_iota(jnp.int32, (length, slots), 1)).astype(jnp.bfloat16)


def gate_and_picking(count, expert_in, router, ids, slot, pitch):
    length = expert_in.shape[0]
    slots = slot.shape[0] * pitch
    whole = pl.BlockSpec(memory_space=pltpu.VMEM)
    return pl.pallas_call(
        functools.partial(gate_kernel, pitch),
        in_specs=[pl.BlockSpec(memory_space=pltpu.SMEM)] + [whole] * 4,
        out_specs=[whole] * 2,
        out_shape=[
            jax.ShapeDtypeStruct((length, 1), jnp.float32),
            jax.ShapeDtypeStruct((length, slots), jnp.bfloat16),
        ],
        compiler_params=pltpu.CompilerParams(vmem_limit_bytes=12 * MIB),
        cost_estimate=SMALL,
        name="gate",
    )(count, expert_in, router.T, ids, slot)


def expert_kernel(parts, span, tile, *refs):
    inputs, (in_a, in_b, out_a, out_b) = refs[:parts], refs[parts : parts + 4]
    outputs, (rows, total) = refs[parts + 4 : 2 * parts + 4], refs[2 * parts + 4 :]
    width = rows.shape[1]
    for number, part in enumerate(inputs):
        rows[number * span : (number + 1) * span, :] = read_part(part, width, span)
    values = rows[...]
    hidden = in_a.shape[1]

    def step(index, carry):
        units = pl.ds(pl.multiple_of(index * tile, tile), tile)
        result = None
        for first, second in ((in_a, out_a), (in_b, out_b)):
            mid = silu(jnp.dot(values, first[:, units], preferred_element_type=jnp.float32)).astype(jnp.bfloat16)
            term = jnp.dot(mid, second[units, :], preferred_element_type=jnp.float32)
            result = term if result is None else result + term

        @pl.when(index == 0)
        def _():
            total[...] = result

        @pl.when(index > 0)
        def _():
            total[...] += result

        return carry

    lax.fori_loop(0, hidden // tile, step, 0)
    for number, part in enumerate(outputs):
        value = total[number * span : (number + 1) * span, :]
        if part.shape[1] != width:
            value = fold(value, part.shape[0] // 2)
        part[...] = value.astype(jnp.bfloat16)


def run_expert(parts, weights, span):
    width = weights[0].shape[0]
    whole = pl.BlockSpec(memory_space=pltpu.VMEM)
    count = len(parts)
    hidden = weights[0].shape[1]
    return pl.pallas_call(
        functools.partial(expert_kernel, count, span, min(1024, hidden)),
        in_specs=[whole] * (count + 4),
        out_specs=[whole] * count,
        out_shape=[jax.ShapeDtypeStruct(parts[0].shape, jnp.bfloat16)] * count,
        scratch_shapes=[
            pltpu.VMEM((span * count, width), jnp.bfloat16),
            pltpu.VMEM((span * count, width), jnp.float32),
        ],
        compiler_params=pltpu.CompilerParams(vmem_limit_bytes=10 * MIB),
        cost_estimate=SMALL,
        name="expert",
    )(*parts, *weights)


def add_kernel(parts, order, span, picking_ref, so_far_ref, gate_ref, *refs):
    inputs, out_ref, results = refs[:parts], refs[parts], refs[parts + 1]
    places = []
    for number, (part, at) in enumerate(zip(inputs, order)):
        results[number * span : (number + 1) * span, :] = read_part(part, results.shape[1], span)
        places.append(picking_ref[:, at * span : (at + 1) * span])
    picking = jnp.concatenate(places, axis=1) if parts > 1 else places[0]
    picked = jnp.dot(picking, results[...], preferred_element_type=jnp.float32)
    out_ref[...] = so_far_ref[...].astype(jnp.float32) + gate_ref[...] * picked


def close_kernel(parts, order, span, picking_ref, so_far_ref, gate_ref, gain_ref, *refs):
    *refs, out_hbm, results, total, out_ref, sems = refs
    add_kernel(parts, order, span, picking_ref, so_far_ref, gate_ref, *refs, total, results)
    copies = []
    for number, start in enumerate(range(0, total.shape[0], BLOCK)):
        rows = slice(start, start + BLOCK)
        out_ref[rows, :] = (normalise(total[rows, :]) * gain_ref[...]).astype(jnp.bfloat16)
        copies.append(
            pltpu.make_async_copy(
                out_ref.at[pl.ds(start, BLOCK), :], out_hbm.at[pl.ds(start, BLOCK), :], sems.at[number]
            )
        )
        copies[-1].start()
    for copy in copies:
        copy.wait()


def add_results(so_far, gate, picking, parts, span, gain=None):
    length, width = so_far.shape
    whole = pl.BlockSpec(memory_space=pltpu.VMEM)
    order, values = tuple(parts), [parts[at] for at in parts]
    scratch = [pltpu.VMEM((span * len(parts), width), jnp.bfloat16)]
    last = gain is not None
    if last:
        scratch.append(pltpu.VMEM((length, width), jnp.float32))
        scratch.append(pltpu.VMEM((length, width), jnp.bfloat16))
        scratch.append(pltpu.SemaphoreType.DMA((length // BLOCK,)))
    return pl.pallas_call(
        functools.partial(close_kernel if last else add_kernel, len(parts), order, span),
        in_specs=[whole] * (3 + last + len(parts)),
        out_specs=pl.BlockSpec(memory_space=pl.ANY) if last else whole,
        out_shape=jax.ShapeDtypeStruct((length, width), jnp.bfloat16 if last else jnp.float32),
        scratch_shapes=scratch,
        compiler_params=pltpu.CompilerParams(vmem_limit_bytes=12 * MIB),
        cost_estimate=SMALL,
        name="finish" if last else "add",
    )(picking, so_far, gate, *([gain] if last else []), *values)


def on_device(frames, frame_counts, expert_ids, conv_kernel, router, w_in, w_out, final_gain):
    _, length, width = frames.shape
    n_dev = lax.axis_size("expert")
    chips = n_dev // 2
    cap = 2 * ((5 * length + 8 * chips - 1) // (8 * chips))
    chip = (lax.axis_index("expert") // 2).astype(jnp.int32).reshape(1)
    other_in = xor_route(w_in, "expert", 1)
    other_out = xor_route(w_out, "expert", 1)
    ids = expert_ids.reshape(1, length)
    gain = final_gain.reshape(1, width)

    if chips <= 8:
        pitch = -(-cap // 16) * 16
        folded = cap % 8 == 4
        own_in, own_out, stream, expert_in, slot, *messages = prepare(
            frames, frame_counts, chip, ids, conv_kernel, w_in, w_out, chips, cap, pitch, chips, folded
        )
        send = lambda part, d: xor_route(part, "expert", 2 * d)
        far = [d for d in range(1, chips) if d >= chips // 2]
        near = [d for d in range(1, chips) if d < chips // 2]
        first, second = far[::2], far[1::2]
        arrived = {d: send(messages[d], d) for d in first}
        other_in, other_out = load(other_in, other_out)
        weights = (own_in, other_in, own_out, other_out)
        for d, part in zip(second, after([messages[d] for d in second], other_in)):
            arrived[d] = send(part, d)
        for d, part in zip(near, [messages[d] for d in near]):
            arrived[d] = send(part, d)
        first_out = run_expert([arrived[d] for d in first], weights, pitch)
        results = {}
        gate, picking = gate_and_picking(frame_counts, expert_in, router, ids, slot, pitch)
        close = run_expert([messages[0]] + after([arrived[d] for d in near], first_out), weights, pitch)
        results[0] = close[0]
        for d, part in zip(first, after(first_out, close)):
            results[d] = send(part, d)
        second_out = run_expert(after([arrived[d] for d in second], (first_out, close)), weights, pitch)
        for d, part in zip(second, second_out):
            results[d] = send(part, d)
        for d, part in zip(near[:2], close[1:3]):
            results[d] = send(part, d)
        for d, part in zip(near[2:], after(close[3:], second_out)):
            results[d] = send(part, d)
        total = add_results(stream, gate, picking, {d: results[d] for d in [0] + first}, pitch)
        total = add_results(total, gate, picking, {d: results[d] for d in near[:2]}, pitch)
        output = add_results(total, gate, picking, {d: results[d] for d in second + near[2:]}, pitch, gain)
    else:
        home = jnp.zeros((1,), jnp.int32)
        own_in, own_out, stream, expert_in, slot, message = prepare(
            frames, frame_counts, home, ids, conv_kernel, w_in, w_out, chips, cap, cap, 1, False
        )
        gate, picking = gate_and_picking(frame_counts, expert_in, router, ids, slot, cap)
        other_in, other_out = load(other_in, other_out)
        (result,) = run_expert([exchange(message, "expert", chips)], (own_in, other_in, own_out, other_out), chips * cap)
        output = add_results(stream, gate, picking, {0: exchange(result, "expert", chips)}, chips * cap, gain)
    return output.reshape(1, length, width)


def solution(mesh):
    return jax.shard_map(
        on_device,
        mesh=mesh,
        in_specs=(
            P(("groups", "expert"), None, None),
            P(("groups", "expert")),
            P(("groups", "expert"), None, None),
            P(),
            P(),
            P(None, "expert"),
            P("expert", None),
            P(),
        ),
        out_specs=P(("groups", "expert"), None, None),
        check_vma=False,
    )
```

```python
import functools

import jax
import jax.numpy as jnp
from jax import lax
from jax.experimental import pallas as pl
from jax.experimental.pallas import tpu as pltpu
from jax.sharding import PartitionSpec as P

LANES = 128
ROWS = 8
BLOCK = 64
EPS = 1e-05
SMALL = pl.CostEstimate(flops=1, bytes_accessed=1, transcendentals=0)
MIB = 1 << 20


def xor_route(block, axis, distance):
    count = lax.axis_size(axis)
    return lax.ppermute(block, axis, [(i, i ^ distance) for i in range(count)])


def after(values, earlier):
    return lax.optimization_barrier((values, earlier))[0]


def exchange(block, axis, chips):
    count = lax.axis_size(axis)
    same_core = [list(range(core, count, 2)) for core in range(2)]
    blocks = block.reshape(chips, block.shape[0] // chips, block.shape[1])
    moved = lax.all_to_all(blocks, axis, split_axis=0, concat_axis=0, tiled=True, axis_index_groups=same_core)
    return moved.reshape(block.shape)


def in_hbm(array):
    return pltpu.with_memory_space_constraint(array, pltpu.HBM)


def silu(value):
    return 0.5 * value * (1.0 + jnp.tanh(0.5 * value))


def fold(values, rows):
    half = values.shape[1] // 2
    return jnp.concatenate([values[:rows, :half], values[:rows, half:]], axis=0)


def unfold(values):
    rows = values.shape[0] // 2
    values = values.astype(jnp.float32)
    return jnp.concatenate([values[:rows, :], values[rows:, :]], axis=1)


def pad_rows(values, rows):
    missing = rows - values.shape[0]
    if not missing:
        return values
    return jnp.concatenate([values, jnp.zeros((missing, values.shape[1]), values.dtype)], axis=0)


def read_part(part, width, pitch):
    values = part[...]
    if values.shape[1] == width:
        return values
    return pad_rows(unfold(values), pitch).astype(jnp.bfloat16)


def normalise(values):
    mean = jnp.mean(values, axis=-1, keepdims=True)
    centred = values - mean
    variance = jnp.mean(centred * centred, axis=-1, keepdims=True)
    return centred * lax.rsqrt(variance + EPS)


def pre_kernel(cap, pitch, count_ref, me_ref, frames_hbm, ids_hbm, taps_hbm, in_hbm, out_hbm, *rest):
    in_ref, out_ref, stream_ref, expert_in_ref, slot_ref, *rest = rest
    *message_refs, frames_ref, taps_ref, ids_ref, padded, taps_by_row, weights, pieces, conv = rest[:-4]
    frame_sems, taps_sem, ids_sem, weight_sems = rest[-4:]
    length, width = frames_ref.shape
    taps = taps_ref.shape[0]
    reach = taps // 2
    groups = width // LANES
    count = count_ref[0]

    frame_copies = [
        pltpu.make_async_copy(
            frames_hbm.at[0, pl.ds(start, BLOCK), :], frames_ref.at[pl.ds(start, BLOCK), :], frame_sems.at[number]
        )
        for number, start in enumerate(range(0, length, BLOCK))
    ]
    taps_copy = pltpu.make_async_copy(taps_hbm, taps_ref, taps_sem)
    for copy in frame_copies:
        copy.start()
    taps_copy.start()
    ids_copy = pltpu.make_async_copy(ids_hbm, ids_ref, ids_sem)
    ids_copy.start()
    weight_copies = [
        pltpu.make_async_copy(in_hbm, in_ref, weight_sems.at[0]),
        pltpu.make_async_copy(out_hbm, out_ref, weight_sems.at[1]),
    ]
    phases = 4
    depth = weights.shape[1] // groups
    edge = jnp.zeros((reach * groups, LANES), jnp.float32)
    padded[: reach * groups, :] = edge
    tail = (reach + length) * groups
    padded[tail:, :] = jnp.zeros((padded.shape[0] - tail, LANES), jnp.float32)
    taps_by_row[taps * groups :, :] = jnp.zeros(((phases * depth - taps) * groups, LANES), jnp.float32)
    taps_copy.wait()
    for group in range(groups):
        lanes = slice(group * LANES, (group + 1) * LANES)
        taps_by_row[pl.ds(group, taps, stride=groups), :] = taps_ref[:, lanes]
    for step in range(depth):
        w = [taps_by_row[(phases * step + i) * groups : (phases * step + i + 1) * groups, :] for i in range(phases)]
        halves = ((w[0] + w[1], w[2] + w[3]), (w[0], w[2]), (w[1], w[3]))
        for number, (even, odd) in enumerate(halves):
            for kind, value in enumerate((even + odd, even, odd)):
                weights[3 * number + kind, step * groups : (step + 1) * groups, :] = value

    for number, start in enumerate(range(0, length, BLOCK)):
        frame_copies[number].wait()
        values = frames_ref[start : start + BLOCK, :].astype(jnp.float32)
        position = start + lax.broadcasted_iota(jnp.int32, (BLOCK, 1), 0)
        normed = jnp.where(position < count, normalise(values), 0.0)
        for group in range(groups):
            lanes = slice(group * LANES, (group + 1) * LANES)
            padded[pl.ds((reach + start) * groups + group, BLOCK, stride=groups), :] = normed[:, lanes]
    for copy in weight_copies:
        copy.start()

    def split(index, carry):
        base = pl.multiple_of(index * (phases * ROWS * groups), phases * ROWS * groups)
        here = pl.multiple_of(index * (ROWS * groups), ROWS * groups)
        p = [padded[pl.ds(base + i * groups, groups), :] for i in range(phases * ROWS + 3)]
        pairs = 2 * ROWS + 1
        streams = (
            [p[2 * i + 1] for i in range(pairs)],
            [p[2 * i] - p[2 * i + 1] for i in range(pairs)],
            [p[2 * i + 2] - p[2 * i + 1] for i in range(pairs)],
        )
        for number, q in enumerate(streams):
            for row in range(ROWS):
                trio = (q[2 * row + 1], q[2 * row] - q[2 * row + 1], q[2 * row + 2] - q[2 * row + 1])
                for kind, value in enumerate(trio):
                    pieces[3 * number + kind, pl.ds(here + row * groups, groups), :] = value
        return carry

    lax.fori_loop(0, pieces.shape[1] // (ROWS * groups), split, 0)

    def correlate(index, carry):
        here = pl.multiple_of(index * (ROWS * groups), ROWS * groups)
        base = pl.multiple_of(index * (phases * ROWS * groups), phases * ROWS * groups)

        def piece(number):
            window = [pieces[number, pl.ds(here + i * groups, groups), :] for i in range(ROWS + depth - 1)]
            sums = None
            for step in range(depth):
                weight = weights[number, step * groups : (step + 1) * groups, :]
                terms = [weight * window[row + step] for row in range(ROWS)]
                sums = terms if sums is None else [a + b for a, b in zip(sums, terms)]
            return sums

        shared = piece(0)
        common = [[a + b for a, b in zip(shared, piece(1 + kind))] for kind in range(2)]
        for parity in range(2):
            shared = piece(3 + 3 * parity)
            for kind in range(2):
                last = piece(4 + 3 * parity + kind)
                for row in range(ROWS):
                    at = base + (phases * row + 2 * kind + parity) * groups
                    conv[pl.ds(at, groups), :] = (shared[row] + last[row]) + common[kind][row]
        return carry

    lax.fori_loop(0, length // (phases * ROWS), correlate, 0)

    for start in range(0, length, BLOCK):
        rows = slice(start, start + BLOCK)
        mixed = jnp.concatenate(
            [conv[pl.ds(start * groups + group, BLOCK, stride=groups), :] for group in range(groups)], axis=1
        )
        stream = (frames_ref[rows, :].astype(jnp.float32) + silu(mixed)).astype(jnp.bfloat16)
        stream_ref[rows, :] = stream
        expert_in_ref[rows, :] = normalise(stream.astype(jnp.float32)).astype(jnp.bfloat16)

    chips = slot_ref.shape[0]
    ids_copy.wait()
    ids = ids_ref[...] ^ me_ref[0]
    at = lax.broadcasted_iota(jnp.int32, (chips, length), 1)
    chosen = (ids == lax.broadcasted_iota(jnp.int32, (chips, length), 0)) & (at < count)
    earlier = lax.broadcasted_iota(jnp.int32, (length, length), 0) < lax.broadcasted_iota(
        jnp.int32, (length, length), 1
    )
    before = jnp.dot(
        chosen.astype(jnp.bfloat16), earlier.astype(jnp.bfloat16), preferred_element_type=jnp.float32
    )
    rank = jnp.sum(jnp.where(chosen, before, 0.0), axis=0, keepdims=True).astype(jnp.int32)
    sent = (at[:1] < count) & (rank < cap)
    slot = jnp.where(sent, ids * pitch + rank, -1)
    slot_ref[...] = jnp.broadcast_to(slot, slot_ref.shape)
    slots = chips * pitch
    placing = (slot == lax.broadcasted_iota(jnp.int32, (slots, length), 0)).astype(jnp.bfloat16)
    span = slots // len(message_refs)
    folded = message_refs[0].shape[1] != width
    part = width // 4
    for start in range(0, width // 2 if folded else width, part):
        placed = [
            jnp.dot(placing, expert_in_ref[:, at : at + part], preferred_element_type=jnp.float32)
            for at in ((start, width // 2 + start) if folded else (start,))
        ]
        for number, message in enumerate(message_refs):
            rows = slice(number * span, (number + 1) * span)
            value = placed[0][rows, :]
            if folded:
                value = fold(jnp.concatenate([value, placed[1][rows, :]], axis=1), cap)
            message[:, start : start + part] = value.astype(jnp.bfloat16)
    for copy in weight_copies:
        copy.wait()


def prepare(frames, count, me, ids, taps, w_in, w_out, chips, cap, pitch, messages, folded):
    _, length, width = frames.shape
    groups = width // LANES
    reach = taps.shape[0] // 2
    whole = pl.BlockSpec(memory_space=pltpu.VMEM)
    anywhere = pl.BlockSpec(memory_space=pl.ANY)
    depth = -(-taps.shape[0] // 4)
    steps = length // 4 + -(-(depth - 1) // ROWS) * ROWS
    span = chips * pitch // messages
    bf16 = jnp.bfloat16
    return pl.pallas_call(
        functools.partial(pre_kernel, cap, pitch),
        in_specs=[pl.BlockSpec(memory_space=pltpu.SMEM)] * 2 + [anywhere] * 5,
        out_specs=[whole] * (5 + messages),
        out_shape=[
            pltpu.VMEM(w_in.shape, bf16),
            pltpu.VMEM(w_out.shape, bf16),
            jax.ShapeDtypeStruct((length, width), bf16),
            jax.ShapeDtypeStruct((length, width), bf16),
            jax.ShapeDtypeStruct((chips, length), jnp.int32),
        ]
        + [jax.ShapeDtypeStruct((2 * cap, width // 2) if folded else (span, width), bf16)] * messages,
        scratch_shapes=[
            pltpu.VMEM((length, width), bf16),
            pltpu.VMEM(taps.shape, jnp.float32),
            pltpu.VMEM(ids.shape, jnp.int32),
            pltpu.VMEM(((4 * steps + 8) * groups, LANES), jnp.float32),
            pltpu.VMEM((4 * depth * groups, LANES), jnp.float32),
            pltpu.VMEM((9, depth * groups, LANES), jnp.float32),
            pltpu.VMEM((9, steps * groups, LANES), jnp.float32),
            pltpu.VMEM((length * groups, LANES), jnp.float32),
            pltpu.SemaphoreType.DMA((length // BLOCK,)),
            pltpu.SemaphoreType.DMA,
            pltpu.SemaphoreType.DMA,
            pltpu.SemaphoreType.DMA((2,)),
        ],
        compiler_params=pltpu.CompilerParams(vmem_limit_bytes=12 * MIB),
        cost_estimate=SMALL,
        name="prepare",
    )(count, me, in_hbm(frames), in_hbm(ids), in_hbm(taps), in_hbm(w_in), in_hbm(w_out))


def load_kernel(count, *refs):
    sources, targets, sems = refs[:count], refs[count : 2 * count], refs[2 * count]
    copies = [pltpu.make_async_copy(a, b, sems.at[i]) for i, (a, b) in enumerate(zip(sources, targets))]
    for copy in copies:
        copy.start()
    for copy in copies:
        copy.wait()


def load(*arrays):
    count = len(arrays)
    return pl.pallas_call(
        functools.partial(load_kernel, count),
        in_specs=[pl.BlockSpec(memory_space=pl.ANY)] * count,
        out_specs=[pl.BlockSpec(memory_space=pltpu.VMEM)] * count,
        out_shape=[pltpu.VMEM(array.shape, array.dtype) for array in arrays],
        scratch_shapes=[pltpu.SemaphoreType.DMA((count,))],
        compiler_params=pltpu.CompilerParams(vmem_limit_bytes=4 * MIB),
        cost_estimate=SMALL,
        name="load",
    )(*[in_hbm(array) for array in arrays])


def gate_kernel(pitch, count_ref, expert_in_ref, router_ref, ids_ref, slot_ref, gate_ref, picking_ref):
    length = expert_in_ref.shape[0]
    experts = router_ref.shape[0]
    slots = picking_ref.shape[1]
    logits = lax.dot_general(
        expert_in_ref[...], router_ref[...], (((1,), (1,)), ((), ())), preferred_element_type=jnp.float32
    )
    ids = jnp.broadcast_to(ids_ref[...].astype(jnp.float32), (experts, length)).T
    position = lax.broadcasted_iota(jnp.int32, (length, experts), 0)
    column = lax.broadcasted_iota(jnp.int32, (length, experts), 1).astype(jnp.float32)
    chosen = (ids == column) & (position < count_ref[0])
    logit = jnp.sum(jnp.where(chosen, logits, 0.0), axis=1, keepdims=True)
    gate_ref[...] = 0.5 / (1.0 + jnp.exp(-logit))
    slot = slot_ref[...].astype(jnp.float32).T[:, :1].astype(jnp.int32)
    picking_ref[...] = (slot == lax.broadcasted_iota(jnp.int32, (length, slots), 1)).astype(jnp.bfloat16)


def gate_and_picking(count, expert_in, router, ids, slot, pitch):
    length = expert_in.shape[0]
    slots = slot.shape[0] * pitch
    whole = pl.BlockSpec(memory_space=pltpu.VMEM)
    return pl.pallas_call(
        functools.partial(gate_kernel, pitch),
        in_specs=[pl.BlockSpec(memory_space=pltpu.SMEM)] + [whole] * 4,
        out_specs=[whole] * 2,
        out_shape=[
            jax.ShapeDtypeStruct((length, 1), jnp.float32),
            jax.ShapeDtypeStruct((length, slots), jnp.bfloat16),
        ],
        compiler_params=pltpu.CompilerParams(vmem_limit_bytes=12 * MIB),
        cost_estimate=SMALL,
        name="gate",
    )(count, expert_in, router.T, ids, slot)


def expert_kernel(parts, span, tile, *refs):
    inputs, (in_a, in_b, out_a, out_b) = refs[:parts], refs[parts : parts + 4]
    outputs, (rows, total) = refs[parts + 4 : 2 * parts + 4], refs[2 * parts + 4 :]
    width = rows.shape[1]
    for number, part in enumerate(inputs):
        rows[number * span : (number + 1) * span, :] = read_part(part, width, span)
    values = rows[...]
    hidden = in_a.shape[1]

    def step(index, carry):
        units = pl.ds(pl.multiple_of(index * tile, tile), tile)
        result = None
        for first, second in ((in_a, out_a), (in_b, out_b)):
            mid = silu(jnp.dot(values, first[:, units], preferred_element_type=jnp.float32)).astype(jnp.bfloat16)
            term = jnp.dot(mid, second[units, :], preferred_element_type=jnp.float32)
            result = term if result is None else result + term

        @pl.when(index == 0)
        def _():
            total[...] = result

        @pl.when(index > 0)
        def _():
            total[...] += result

        return carry

    lax.fori_loop(0, hidden // tile, step, 0)
    for number, part in enumerate(outputs):
        value = total[number * span : (number + 1) * span, :]
        if part.shape[1] != width:
            value = fold(value, part.shape[0] // 2)
        part[...] = value.astype(jnp.bfloat16)


def run_expert(parts, weights, span):
    width = weights[0].shape[0]
    whole = pl.BlockSpec(memory_space=pltpu.VMEM)
    count = len(parts)
    hidden = weights[0].shape[1]
    return pl.pallas_call(
        functools.partial(expert_kernel, count, span, min(2048, hidden)),
        in_specs=[whole] * (count + 4),
        out_specs=[whole] * count,
        out_shape=[jax.ShapeDtypeStruct(parts[0].shape, jnp.bfloat16)] * count,
        scratch_shapes=[
            pltpu.VMEM((span * count, width), jnp.bfloat16),
            pltpu.VMEM((span * count, width), jnp.float32),
        ],
        compiler_params=pltpu.CompilerParams(vmem_limit_bytes=10 * MIB),
        cost_estimate=SMALL,
        name="expert",
    )(*parts, *weights)


def add_kernel(parts, order, span, picking_ref, so_far_ref, gate_ref, *refs):
    inputs, out_ref, results = refs[:parts], refs[parts], refs[parts + 1]
    places = []
    for number, (part, at) in enumerate(zip(inputs, order)):
        results[number * span : (number + 1) * span, :] = read_part(part, results.shape[1], span)
        places.append(picking_ref[:, at * span : (at + 1) * span])
    picking = jnp.concatenate(places, axis=1) if parts > 1 else places[0]
    picked = jnp.dot(picking, results[...], preferred_element_type=jnp.float32)
    out_ref[...] = so_far_ref[...].astype(jnp.float32) + gate_ref[...] * picked


def close_kernel(parts, order, span, picking_ref, so_far_ref, gate_ref, gain_ref, *refs):
    *refs, out_hbm, results, total, out_ref, sems = refs
    add_kernel(parts, order, span, picking_ref, so_far_ref, gate_ref, *refs, total, results)
    copies = []
    for number, start in enumerate(range(0, total.shape[0], BLOCK)):
        rows = slice(start, start + BLOCK)
        out_ref[rows, :] = (normalise(total[rows, :]) * gain_ref[...]).astype(jnp.bfloat16)
        copies.append(
            pltpu.make_async_copy(
                out_ref.at[pl.ds(start, BLOCK), :], out_hbm.at[pl.ds(start, BLOCK), :], sems.at[number]
            )
        )
        copies[-1].start()
    for copy in copies:
        copy.wait()


def add_results(so_far, gate, picking, parts, span, gain=None):
    length, width = so_far.shape
    whole = pl.BlockSpec(memory_space=pltpu.VMEM)
    order, values = tuple(parts), [parts[at] for at in parts]
    scratch = [pltpu.VMEM((span * len(parts), width), jnp.bfloat16)]
    last = gain is not None
    if last:
        scratch.append(pltpu.VMEM((length, width), jnp.float32))
        scratch.append(pltpu.VMEM((length, width), jnp.bfloat16))
        scratch.append(pltpu.SemaphoreType.DMA((length // BLOCK,)))
    return pl.pallas_call(
        functools.partial(close_kernel if last else add_kernel, len(parts), order, span),
        in_specs=[whole] * (3 + last + len(parts)),
        out_specs=pl.BlockSpec(memory_space=pl.ANY) if last else whole,
        out_shape=jax.ShapeDtypeStruct((length, width), jnp.bfloat16 if last else jnp.float32),
        scratch_shapes=scratch,
        compiler_params=pltpu.CompilerParams(vmem_limit_bytes=12 * MIB),
        cost_estimate=SMALL,
        name="finish" if last else "add",
    )(picking, so_far, gate, *([gain] if last else []), *values)


def on_device(frames, frame_counts, expert_ids, conv_kernel, router, w_in, w_out, final_gain):
    _, length, width = frames.shape
    n_dev = lax.axis_size("expert")
    chips = n_dev // 2
    cap = 2 * ((5 * length + 8 * chips - 1) // (8 * chips))
    chip = (lax.axis_index("expert") // 2).astype(jnp.int32).reshape(1)
    other_in = xor_route(w_in, "expert", 1)
    other_out = xor_route(w_out, "expert", 1)
    ids = expert_ids.reshape(1, length)
    gain = final_gain.reshape(1, width)

    if chips <= 8:
        pitch = -(-cap // 16) * 16
        folded = cap % 8 == 4
        own_in, own_out, stream, expert_in, slot, *messages = prepare(
            frames, frame_counts, chip, ids, conv_kernel, w_in, w_out, chips, cap, pitch, chips, folded
        )
        send = lambda part, d: xor_route(part, "expert", 2 * d)
        far = [d for d in range(1, chips) if d >= chips // 2]
        near = [d for d in range(1, chips) if d < chips // 2]
        first, second = far[::2], far[1::2]
        arrived = {d: send(messages[d], d) for d in first}
        other_in, other_out = load(other_in, other_out)
        weights = (own_in, other_in, own_out, other_out)
        for d, part in zip(second, after([messages[d] for d in second], other_in)):
            arrived[d] = send(part, d)
        for d, part in zip(near, [messages[d] for d in near]):
            arrived[d] = send(part, d)
        first_out = run_expert([arrived[d] for d in first], weights, pitch)
        results = {}
        gate, picking = gate_and_picking(frame_counts, expert_in, router, ids, slot, pitch)
        close = run_expert([messages[0]] + after([arrived[d] for d in near], first_out), weights, pitch)
        results[0] = close[0]
        for d, part in zip(first, after(first_out, close)):
            results[d] = send(part, d)
        second_out = run_expert(after([arrived[d] for d in second], (first_out, close)), weights, pitch)
        for d, part in zip(second, second_out):
            results[d] = send(part, d)
        for d, part in zip(near[:2], close[1:3]):
            results[d] = send(part, d)
        for d, part in zip(near[2:], after(close[3:], second_out)):
            results[d] = send(part, d)
        total = add_results(stream, gate, picking, {d: results[d] for d in [0] + first}, pitch)
        total = add_results(total, gate, picking, {d: results[d] for d in near[:2]}, pitch)
        output = add_results(total, gate, picking, {d: results[d] for d in second + near[2:]}, pitch, gain)
    else:
        home = jnp.zeros((1,), jnp.int32)
        own_in, own_out, stream, expert_in, slot, message = prepare(
            frames, frame_counts, home, ids, conv_kernel, w_in, w_out, chips, cap, cap, 1, False
        )
        gate, picking = gate_and_picking(frame_counts, expert_in, router, ids, slot, cap)
        other_in, other_out = load(other_in, other_out)
        (result,) = run_expert([exchange(message, "expert", chips)], (own_in, other_in, own_out, other_out), chips * cap)
        output = add_results(stream, gate, picking, {0: exchange(result, "expert", chips)}, chips * cap, gain)
    return output.reshape(1, length, width)


def solution(mesh):
    return jax.shard_map(
        on_device,
        mesh=mesh,
        in_specs=(
            P(("groups", "expert"), None, None),
            P(("groups", "expert")),
            P(("groups", "expert"), None, None),
            P(),
            P(),
            P(None, "expert"),
            P("expert", None),
            P(),
        ),
        out_specs=P(("groups", "expert"), None, None),
        check_vma=False,
    )
```
